128 devices in a mesh: space: 8 (over x, y_hi), mode: 16 (over z, y_lo, core).
Axes of the slice: x: 4, y: 4 (y_hi: 2, y_lo: 2; y = y_hi * 2 + y_lo), z: 4, core: 2. Of those that a mesh axis runs over, the one named last changes fastest.
Arguments:
- displacement: bfloat16 [256, 64, 4096], P('mode', 'space'), may hold values from -0.29882812 to 0.29882812
- direction: bfloat16 [256, 64, 4096], P('mode', 'space'), may hold values from -0.29882812 to 0.29882812
- quad_nodes: float32 [512, 8], replicated, may hold values from -3 to 3
- quad_weights: float32 [512], replicated, may hold values from 0.0009765625 to 0.00390625
- gap_nominal: float32 [512], replicated, may hold values from 1 to 2
- pressure_load: float32 [512], replicated, may hold values from 0.2 to 0.6
- degrees: int32 [256, 8], replicated, may hold values from 0 to 4, as said below
Outputs:
- residual: float32 [256, 64, 4096], P('mode', 'space')
- tangent: float32 [256, 64, 4096], P('mode', 'space')
The draws below stay inside these ranges and needn't reach their ends.
Inputs may be any that keep to these rules, and one draw needn't show every extreme that they name: `degrees`: the rows are distinct multi-indices of total degree at most 4 in order of non-decreasing total degree: every multi-index of a total degree appears before any of a higher one, and all of each lower total degree are present.
All inputs are finite; a program needn't handle non-finite values.
Results may differ from the reference program's by a relative error of at most 0.007.
Values may be sent and summed in bfloat16 or wider, within the bound.
No kernel may reach another device: no remote copies, remote signals or barrier semaphores. Data moves between devices by JAX's collectives and lax.ppermute only.
A program may use at most 128 MiB of HBM per device.

```python
import math
import jax
import jax.numpy as jnp
import numpy as np
from jax import lax

MODES = 256
QUAD = 512
PARAMS = 8
NY = 4096
ROWS_DEV = 8
NX = 64


def spread_degree(total, slots):
    if slots == 1:
        return [[total]]
    listed = []
    for first in range(total, -1, -1):
        for rest in spread_degree(total - first, slots - 1):
            listed.append([first] + rest)
    return listed


def graded_table(count, params):
    listed = []
    for total in range(0, 5):
        listed.extend(spread_degree(total, params))
    return np.array(listed[:count], dtype=np.int32)


def draw_degrees(key, part):
    fixed_rows = jnp.asarray(graded_table(MODES, PARAMS))
    order = jax.random.permutation(jax.random.fold_in(key, 17), PARAMS).astype(jnp.int32)
    return jnp.take(fixed_rows, order, axis=1).astype(jnp.int32)


def steps_of(stream_key, shape, cuts, least, high):
    factor_of, own = 1.0, jax.random.fold_in(stream_key, 6)
    for axis_at, blocks in cuts:
        steps = jnp.exp(jax.random.uniform(jax.random.fold_in(own, axis_at), (blocks,), jnp.float32, least / len(cuts), high / len(cuts)))
        factor_of = factor_of * jnp.repeat(steps, shape[axis_at] // blocks).reshape([-1 if axis == axis_at else 1 for axis in range(len(shape))])
    return factor_of


def noise(rng, shape, spread, limit, shards=(), kind=jnp.bfloat16):
    entries = spread * jax.random.normal(rng, shape, jnp.float32)
    if shards:
        entries = entries * steps_of(rng, shape, shards, -0.22, 0.18)
    return jnp.clip(entries, -limit, limit).astype(kind)


def setup_inputs(seed: int = 0) -> dict:
    streams_of = jax.random.split(jax.random.key(seed), 8)
    displacement = noise(streams_of[0], (MODES, NX, NY), 0.05, 0.29882812, ((0, 16), (1, 8)))
    direction = noise(streams_of[1], (MODES, NX, NY), 0.05, 0.29882812, ((0, 16), (1, 8)))
    quad_nodes = noise(streams_of[2], (QUAD, PARAMS), 1.0, 3.0, (), jnp.float32)
    quad_weights = jnp.clip(jnp.exp(jax.random.uniform(streams_of[3], (QUAD,), jnp.float32, math.log(0.0009765625), math.log(0.00390625))), 0.0009765625, 0.00390625)
    gap_nominal = jnp.clip(jnp.exp(jax.random.uniform(streams_of[4], (QUAD,), jnp.float32, math.log(1.0), math.log(2.0))), 1.0, 2.0)
    pressure_load = jnp.clip(jnp.exp(jax.random.uniform(streams_of[5], (QUAD,), jnp.float32, math.log(0.2), math.log(0.6))), 0.2, 0.6)
    degrees = draw_degrees(jax.random.fold_in(streams_of[7], 71), 0)
    return {"displacement": displacement, "direction": direction, "quad_nodes": quad_nodes, "quad_weights": quad_weights, "gap_nominal": gap_nominal, "pressure_load": pressure_load, "degrees": degrees}


HALF_ROOT = 0.7071067811865476
THIRD_NORM = 0.4082482904638631
FOURTH_NORM = 0.2041241452319315
FLOOR = 0.3
STEEP = 4.0
STIFF = 0.1


def basis(quad_nodes, degrees):
    points = quad_nodes[None, :, :]
    degree_grid = degrees[:, None, :]
    square = points * points
    third = (square * points - 3.0 * points) * THIRD_NORM
    fourth = (square * square - 6.0 * square + 3.0) * FOURTH_NORM
    second = (square - 1.0) * HALF_ROOT
    factor = jnp.where(degree_grid == 0, 1.0,
                       jnp.where(degree_grid == 1, points,
                                 jnp.where(degree_grid == 2, second,
                                           jnp.where(degree_grid == 3, third, fourth))))
    return jnp.prod(factor, axis=2).astype(jnp.bfloat16)


def quad_forces(pieces, table, table_t, quad_weights, gap_nominal, pressure_load):
    count = pieces.shape[1]
    height = pieces.shape[2]
    breadth = pieces.shape[3]
    first = pieces[0].reshape(count, height * breadth)
    second = pieces[1].reshape(count, height * breadth)
    values_q = jnp.dot(table_t, first, preferred_element_type=jnp.float32)
    probe_q = jnp.dot(table_t, second, preferred_element_type=jnp.float32)
    shifted = STEEP * (gap_nominal[:, None] - values_q - FLOOR)
    gap = FLOOR + jax.nn.softplus(shifted) / STEEP
    pressure = pressure_load[:, None] / (gap * gap)
    slope_q = 2.0 * pressure_load[:, None] * jax.nn.sigmoid(shifted) / (gap * gap * gap)
    weighted = (quad_weights[:, None] * pressure).astype(jnp.bfloat16)
    weighted_t = (quad_weights[:, None] * slope_q * probe_q).astype(jnp.bfloat16)
    force = jnp.dot(table, weighted, preferred_element_type=jnp.float32).astype(jnp.bfloat16)
    force_t = jnp.dot(table, weighted_t, preferred_element_type=jnp.float32).astype(jnp.bfloat16)
    return jnp.stack([force, force_t]).reshape(2, count, height, breadth)


def biharm(padded):
    height = padded.shape[-2] - 4
    breadth = padded.shape[-1] - 4

    def offset_view(down, across):
        return padded[..., 2 + down:2 + down + height, 2 + across:2 + across + breadth]

    center = 20.0 * offset_view(0, 0)
    near = offset_view(1, 0) + offset_view(-1, 0) + offset_view(0, 1) + offset_view(0, -1)
    corner = offset_view(1, 1) + offset_view(1, -1) + offset_view(-1, 1) + offset_view(-1, -1)
    far = offset_view(2, 0) + offset_view(-2, 0) + offset_view(0, 2) + offset_view(0, -2)
    return center - 8.0 * near + 2.0 * corner + far


def reference(displacement, direction, quad_nodes, quad_weights, gap_nominal, pressure_load, degrees):
    table = basis(quad_nodes, degrees)
    table_t = table.T

    def one_block(index):
        start = (index * ROWS_DEV).astype(jnp.int32)
        blocks = jnp.stack([lax.dynamic_slice_in_dim(displacement, start, ROWS_DEV, 1),
                            lax.dynamic_slice_in_dim(direction, start, ROWS_DEV, 1)])
        return quad_forces(blocks, table, table_t, quad_weights, gap_nominal, pressure_load)

    forces = lax.map(one_block, jnp.arange(NX // ROWS_DEV, dtype=jnp.int32))
    forces = jnp.moveaxis(forces, 0, 2).reshape(2, MODES, NX, NY)

    def one_mode(index):
        fields = jnp.stack([displacement[index], direction[index]]).astype(jnp.float32)
        padded = jnp.pad(fields, ((0, 0), (2, 2), (2, 2)))
        return STIFF * biharm(padded)

    stencil = lax.map(one_mode, jnp.arange(MODES, dtype=jnp.int32))
    stencil = jnp.moveaxis(stencil, 0, 1)
    results = stencil - forces.astype(jnp.float32)
    return results[0], results[1]
```

```python
import functools

import jax
import jax.numpy as jnp
from jax import lax
from jax.experimental import pallas as pl
from jax.experimental.pallas import tpu as pltpu
from jax.sharding import PartitionSpec as P

HALF_ROOT = 0.7071067811865476
THIRD_NORM = 0.4082482904638631
FOURTH_NORM = 0.2041241452319315
FLOOR = 0.3
STEEP = 4.0
STIFF = 0.1
LOG2E = 1.4426950408889634
LN2 = 0.6931471805599453
MIB = 1 << 20
F32 = jnp.float32
BF16 = jnp.bfloat16


def basis(quad_nodes, degrees):
    points = quad_nodes[None, :, :]
    degree_grid = degrees[:, None, :]
    square = points * points
    third = (square * points - 3.0 * points) * THIRD_NORM
    fourth = (square * square - 6.0 * square + 3.0) * FOURTH_NORM
    second = (square - 1.0) * HALF_ROOT
    factor = jnp.where(
        degree_grid == 0,
        1.0,
        jnp.where(
            degree_grid == 1,
            points,
            jnp.where(degree_grid == 2, second, jnp.where(degree_grid == 3, third, fourth)),
        ),
    )
    return jnp.prod(factor, axis=2).astype(BF16)


def iotas(shape):
    return lax.broadcasted_iota(jnp.int32, shape, 0), lax.broadcasted_iota(jnp.int32, shape, 1)


def one_hot(hit):
    return jnp.where(hit, 1.0, 0.0).astype(BF16)


def pack_kernel(dests, disp_ref, dir_ref, send_ref, low_ref, high_ref):
    modes, rows, width = disp_ref.shape
    both = 2 * modes
    size = both * rows
    to, frm = iotas((size, size))
    perm = one_hot(frm == (to % both) * rows + to // both)
    each = width // dests
    for d in range(dests):
        cols = pl.ds(d * each, each)
        fields = jnp.concatenate(
            [disp_ref[:, :, cols].reshape(modes * rows, each), dir_ref[:, :, cols].reshape(modes * rows, each)], axis=0
        )
        moved = jnp.dot(perm, fields, preferred_element_type=F32).astype(BF16).reshape(rows, both, each)
        send_ref[d] = moved
        low_ref[:, :, cols] = moved[:2]
        high_ref[:, :, cols] = moved[rows - 2 :]


def pack(displacement, direction, count, dests=4):
    modes, rows, width = displacement.shape
    each = width // count
    both = 2 * modes
    field = pl.BlockSpec((modes, rows, dests * each), lambda i: (0, 0, i))
    edge = pl.BlockSpec((2, both, dests * each), lambda i: (0, 0, i))
    return pl.pallas_call(
        functools.partial(pack_kernel, dests),
        grid=(count // dests,),
        in_specs=[field, field],
        out_specs=[pl.BlockSpec((dests, rows, both, each), lambda i: (i, 0, 0, 0)), edge, edge],
        out_shape=[
            jax.ShapeDtypeStruct((count, rows, both, each), BF16),
            jax.ShapeDtypeStruct((2, both, width), BF16),
            jax.ShapeDtypeStruct((2, both, width), BF16),
        ],
        compiler_params=pltpu.CompilerParams(vmem_limit_bytes=16 * MIB),
        cost_estimate=pl.CostEstimate(flops=2 * (2 * modes * rows) ** 2 * width, bytes_accessed=5 * MIB, transcendentals=0),
        name="pack",
    )(displacement, direction)


def quad_kernel(chunk, got_ref, table_t_ref, table_w_ref, shift_ref, out_ref, w_ref, wt_ref):
    count, _, both, width = got_ref.shape
    modes = both // 2
    quad = table_t_ref.shape[0]
    total = count * modes
    disp = got_ref[:, 0, :modes, :].reshape(total, width)
    dire = got_ref[:, 0, modes:, :].reshape(total, width)
    for q in range(quad // chunk):
        at = pl.ds(q * chunk, chunk)
        left = table_t_ref[at, :]
        shift = shift_ref[at, :]
        shift = jnp.concatenate([shift] * (width // shift.shape[1]), axis=1)
        s = shift - STEEP * jnp.dot(left, disp, preferred_element_type=F32)
        probe = jnp.dot(left, dire, preferred_element_type=F32)
        e = jnp.exp2(jnp.abs(s) * (-LOG2E))
        one = 1.0 + e
        gap = (jnp.maximum(s, 0.0) * (1.0 / STEEP) + FLOOR) + jnp.log2(one) * (LN2 / STEEP)
        sig = jnp.where(s >= 0.0, 1.0, e) * pl.reciprocal(one, approx=True)
        inv = pl.reciprocal(gap, approx=True)
        square = inv * inv
        w_ref[at, :] = square.astype(BF16)
        wt_ref[at, :] = (sig * (inv + inv) * square * probe).astype(BF16)
    table_w = table_w_ref[...]
    force = jnp.dot(table_w, w_ref[...], preferred_element_type=F32).astype(BF16)
    force_t = jnp.dot(table_w, wt_ref[...], preferred_element_type=F32).astype(BF16)
    out_ref[:, 0, :modes, :] = force.reshape(count, modes, width)
    out_ref[:, 0, modes:, :] = force_t.reshape(count, modes, width)


def quad_forces(got, table_t, table_w, shift):
    count, rows, both, width = got.shape
    quad, total = table_t.shape
    block = pl.BlockSpec((count, 1, both, width), lambda i: (0, i, 0, 0))
    return pl.pallas_call(
        functools.partial(quad_kernel, 128),
        grid=(rows,),
        in_specs=[
            block,
            pl.BlockSpec((quad, total), lambda i: (0, 0)),
            pl.BlockSpec((total, quad), lambda i: (0, 0)),
            pl.BlockSpec(shift.shape, lambda i: (0, 0)),
        ],
        out_specs=block,
        out_shape=jax.ShapeDtypeStruct(got.shape, BF16),
        scratch_shapes=[pltpu.VMEM((quad, width), BF16), pltpu.VMEM((quad, width), BF16)],
        compiler_params=pltpu.CompilerParams(vmem_limit_bytes=16 * MIB),
        cost_estimate=pl.CostEstimate(
            flops=8 * quad * total * rows * width, bytes_accessed=5 * MIB, transcendentals=4 * quad * rows * width
        ),
        name="quad_forces",
    )(got, table_t, table_w, shift)


def stencil_kernel(chunk, x_ref, above_ref, below_ref, out_ref, side_ref):
    modes, rows, width = x_ref.shape
    size = modes * rows
    edge = 2 * modes
    span = size + 2 * edge
    to, frm = iotas((size, span))
    late = frm - size
    outer = late // modes
    row_in = jnp.where(late < 0, frm % rows, jnp.where(outer < 2, outer - 2, outer + rows - 2))
    mode_in = jnp.where(late < 0, frm // rows, late % modes)
    gap = jnp.abs(row_in - to % rows)
    same = mode_in == to // rows

    def weights(zero, one, two):
        value = jnp.where(gap == 0, zero, jnp.where(gap == 1, one, jnp.where(gap == 2, two, 0.0)))
        return jnp.where(same, value, 0.0).astype(BF16)

    centre = weights(20.0, -8.0, 1.0)
    side = weights(-8.0, 2.0, 0.0)
    for c in range(width // chunk):
        cols = pl.ds(c * chunk, chunk)
        operand = jnp.concatenate(
            [
                x_ref[:, :, cols].reshape(size, chunk),
                above_ref[:, :, cols].reshape(edge, chunk),
                below_ref[:, :, cols].reshape(edge, chunk),
            ],
            axis=0,
        )
        out_ref[:, :, cols] = jnp.dot(centre, operand, preferred_element_type=F32).reshape(modes, rows, chunk)
        side_ref[:, :, cols] = jnp.dot(side, operand, preferred_element_type=F32).reshape(modes, rows, chunk)
    lane = lax.broadcasted_iota(jnp.int32, (rows, width), 1)

    def one_mode(m, _):
        x = x_ref[m].astype(F32)
        y = side_ref[m]

        def from_right(v):
            return jnp.where(lane == width - 1, 0.0, pltpu.roll(v, width - 1, 1))

        def from_left(v):
            return jnp.where(lane == 0, 0.0, pltpu.roll(v, 1, 1))

        total = out_ref[m] + from_right(y + from_right(x)) + from_left(y + from_left(x))
        out_ref[m] = STIFF * total
        return 0

    lax.fori_loop(0, modes, one_mode, 0)


def stencil(x, above, below, field):
    modes, rows, width = x.shape
    edge = pl.BlockSpec((2, modes, width), lambda i: (0, field, 0))
    whole = pl.BlockSpec((modes, rows, width), lambda i: (0, 0, 0))
    return pl.pallas_call(
        functools.partial(stencil_kernel, 512),
        grid=(1,),
        in_specs=[whole, edge, edge],
        out_specs=whole,
        out_shape=jax.ShapeDtypeStruct(x.shape, F32),
        scratch_shapes=[pltpu.VMEM(x.shape, F32)],
        compiler_params=pltpu.CompilerParams(vmem_limit_bytes=20 * MIB),
        cost_estimate=pl.CostEstimate(flops=4 * 128 * 192 * 4096 * 2, bytes_accessed=4 * MIB, transcendentals=0),
        name="stencil",
    )(x, above, below)


def merge_kernel(sources, force_ref, res_ref, tan_ref, res_out, tan_out):
    _, rows, both, each = force_ref.shape
    modes = both // 2
    size = both * rows
    to, frm = iotas((size, size))
    perm = one_hot(frm == (to % rows) * both + to // rows)
    for d in range(sources):
        cols = pl.ds(d * each, each)
        moved = jnp.dot(perm, force_ref[d].reshape(size, each), preferred_element_type=F32)
        moved = moved.reshape(both, rows, each)
        res_out[:, :, cols] = res_ref[:, :, cols] - moved[:modes]
        tan_out[:, :, cols] = tan_ref[:, :, cols] - moved[modes:]


def merge(force, res, tan, sources=4):
    count, rows, both, each = force.shape
    modes = both // 2
    field = pl.BlockSpec((modes, rows, sources * each), lambda i: (0, 0, i))
    return pl.pallas_call(
        functools.partial(merge_kernel, sources),
        grid=(count // sources,),
        in_specs=[pl.BlockSpec((sources, rows, both, each), lambda i: (i, 0, 0, 0)), field, field],
        out_specs=[field, field],
        out_shape=[jax.ShapeDtypeStruct(res.shape, F32)] * 2,
        compiler_params=pltpu.CompilerParams(vmem_limit_bytes=20 * MIB),
        cost_estimate=pl.CostEstimate(flops=2 * (both * rows) ** 2 * each * count, bytes_accessed=10 * MIB, transcendentals=0),
        name="merge",
    )(force, res, tan)


def shards(displacement, direction, quad_nodes, quad_weights, gap_nominal, pressure_load, degrees):
    count = lax.axis_size("mode")
    bands = lax.axis_size("space")
    send, low, high = pack(displacement, direction, count)
    got = lax.all_to_all(send, "mode", split_axis=0, concat_axis=0, tiled=True)
    above = lax.ppermute(high, "space", [(i, i + 1) for i in range(bands - 1)])
    below = lax.ppermute(low, "space", [(i + 1, i) for i in range(bands - 1)])
    table = basis(quad_nodes, degrees)
    table_w = (table.astype(F32) * (quad_weights * pressure_load)[None, :]).astype(BF16)
    shift = jnp.broadcast_to((STEEP * (gap_nominal - FLOOR))[:, None], (gap_nominal.shape[0], 128))
    force = quad_forces(got, table.T, table_w, shift)
    back = lax.all_to_all(force, "mode", split_axis=0, concat_axis=0, tiled=True)
    res = stencil(displacement, above, below, 0)
    tan = stencil(direction, above, below, 1)
    return tuple(merge(back, res, tan))


def solution(mesh):
    in_specs = (P("mode", "space", None), P("mode", "space", None), P(), P(), P(), P(), P())
    out_specs = (P("mode", "space", None), P("mode", "space", None))
    return jax.shard_map(shards, mesh=mesh, in_specs=in_specs, out_specs=out_specs, check_vma=False)
```

```python
import functools

import jax
import jax.numpy as jnp
from jax import lax
from jax.experimental import pallas as pl
from jax.experimental.pallas import tpu as pltpu
from jax.sharding import PartitionSpec as P

HALF_ROOT = 0.7071067811865476
THIRD_NORM = 0.4082482904638631
FOURTH_NORM = 0.2041241452319315
FLOOR = 0.3
STEEP = 4.0
STIFF = 0.1
LOG2E = 1.4426950408889634
LN2 = 0.6931471805599453
MIB = 1 << 20
VMEM = 24 * MIB
F32 = jnp.float32
BF16 = jnp.bfloat16
HBM = pltpu.HBM


def basis(quad_nodes, degrees):
    points = quad_nodes[None, :, :]
    degree_grid = degrees[:, None, :]
    square = points * points
    third = (square * points - 3.0 * points) * THIRD_NORM
    fourth = (square * square - 6.0 * square + 3.0) * FOURTH_NORM
    second = (square - 1.0) * HALF_ROOT
    factor = jnp.where(
        degree_grid == 0,
        1.0,
        jnp.where(
            degree_grid == 1,
            points,
            jnp.where(degree_grid == 2, second, jnp.where(degree_grid == 3, third, fourth)),
        ),
    )
    return jnp.prod(factor, axis=2).astype(BF16)


def iotas(shape):
    return lax.broadcasted_iota(jnp.int32, shape, 0), lax.broadcasted_iota(jnp.int32, shape, 1)


def one_hot(hit):
    return jnp.where(hit, 1.0, 0.0).astype(BF16)


def pack_kernel(groups, disp_ref, dir_ref, send_ref, in_buf, out_buf, in_sem, out_sem):
    modes, rows, width = disp_ref.shape
    count, _, both, each = send_ref.shape
    size = both * rows
    per = count // groups
    span = per * each

    def loads(g):
        cols = pl.ds(g * span, span)
        return [
            pltpu.make_async_copy(ref.at[:, :, cols], in_buf.at[f, :, :, cols], in_sem.at[f, g])
            for f, ref in enumerate((disp_ref, dir_ref))
        ]

    def store(g):
        at = pl.ds(g * per, per)
        return pltpu.make_async_copy(out_buf.at[at], send_ref.at[at], out_sem.at[g])

    for g in range(groups):
        for copy in loads(g):
            copy.start()
    to, frm = iotas((size, size))
    perm = one_hot(frm == (to % both) * rows + to // both)
    for g in range(groups):
        for copy in loads(g):
            copy.wait()
        for d in range(g * per, (g + 1) * per):
            fields = in_buf[:, :, :, pl.ds(d * each, each)].reshape(size, each)
            moved = jnp.dot(perm, fields, preferred_element_type=F32).astype(BF16)
            out_buf[d] = moved.reshape(rows, both, each)
        store(g).start()
    for g in range(groups):
        store(g).wait()


def pack(displacement, direction, count, groups=8):
    modes, rows, width = displacement.shape
    each = width // count
    both = 2 * modes
    hbm = pl.BlockSpec(memory_space=HBM)
    shape = (count, rows, both, each)
    return pl.pallas_call(
        functools.partial(pack_kernel, groups),
        in_specs=[hbm, hbm],
        out_specs=hbm,
        out_shape=pltpu.HBM(shape, BF16),
        scratch_shapes=[
            pltpu.VMEM((2, modes, rows, width), BF16),
            pltpu.VMEM(shape, BF16),
            pltpu.SemaphoreType.DMA((2, groups)),
            pltpu.SemaphoreType.DMA((groups,)),
        ],
        compiler_params=pltpu.CompilerParams(vmem_limit_bytes=VMEM),
        cost_estimate=pl.CostEstimate(flops=2 * (2 * modes * rows) ** 2 * width, bytes_accessed=4 * MIB, transcendentals=0),
        name="pack",
    )(pltpu.with_memory_space_constraint(displacement, HBM), pltpu.with_memory_space_constraint(direction, HBM))


def quad_kernel(chunk, got_ref, table_t_ref, table_w_ref, shift_ref, out_ref, out_buf, w_ref, out_sem):
    count, rows, both, width = got_ref.shape
    modes = both // 2
    quad = table_t_ref.shape[0]
    total = count * modes

    def store(r):
        return pltpu.make_async_copy(out_buf.at[r], out_ref.at[:, r], out_sem.at[r])

    def one_row(r, _):
        disp = got_ref[:, r, :modes, :].reshape(total, width)
        dire = got_ref[:, r, modes:, :].reshape(total, width)
        for q in range(quad // chunk):
            at = pl.ds(q * chunk, chunk)
            left = table_t_ref[at, :]
            shift = shift_ref[at, :]
            shift = jnp.concatenate([shift] * (width // shift.shape[1]), axis=1)
            s = shift + jnp.dot(left, disp, preferred_element_type=F32)
            probe = jnp.dot(left, dire, preferred_element_type=F32)
            e = jnp.exp2(jnp.minimum(s, 80.0) * LOG2E)
            one = 1.0 + e
            big = jnp.maximum(s, jnp.log2(one) * LN2) + STEEP * FLOOR
            inv = pl.reciprocal(big, approx=True)
            sig = e * pl.reciprocal(one, approx=True)
            square = inv * inv
            w_ref[0, at, :] = square.astype(BF16)
            w_ref[1, at, :] = ((sig * inv) * (square * probe)).astype(BF16)
        table_w = table_w_ref[...]
        for f in range(2):
            force = jnp.dot(table_w, w_ref[f], preferred_element_type=F32).astype(BF16)
            out_buf[r, :, f * modes : (f + 1) * modes, :] = force.reshape(count, modes, width)
        store(r).start()
        return 0

    lax.fori_loop(0, rows, one_row, 0)
    for r in range(rows):
        store(r).wait()


def quad_forces(got, table_t, table_w, shift):
    count, rows, both, width = got.shape
    quad, total = table_t.shape
    hbm = pl.BlockSpec(memory_space=HBM)
    vmem = pl.BlockSpec(memory_space=pltpu.VMEM)
    return pl.pallas_call(
        functools.partial(quad_kernel, 128),
        in_specs=[vmem] * 4,
        out_specs=hbm,
        out_shape=pltpu.HBM(got.shape, BF16),
        scratch_shapes=[
            pltpu.VMEM((rows, count, both, width), BF16),
            pltpu.VMEM((2, quad, width), BF16),
            pltpu.SemaphoreType.DMA((rows,)),
        ],
        compiler_params=pltpu.CompilerParams(vmem_limit_bytes=VMEM),
        cost_estimate=pl.CostEstimate(flops=8589934592, bytes_accessed=4194304, transcendentals=0),
        name="quad_forces",
    )(got, table_t, table_w, shift)


def shifted(v, lane, by):
    width = v.shape[-1]
    inside = lane < width - 1 if by > 0 else lane > 0
    return jnp.where(inside, pltpu.roll(v, width - 1 if by > 0 else 1, 1), 0.0)


def stencil_kernel(chunk, x_ref, above_ref, below_ref, out_ref, inner_ref, side_ref):
    modes, rows, width = x_ref.shape
    size = modes * rows
    to, frm = iotas((size, size))
    gap = jnp.abs(to - frm)
    same = to // rows == frm // rows
    centre = jnp.where(gap == 0, 20.0, jnp.where(gap == 1, -8.0, jnp.where(gap == 2, 1.0, 0.0)))
    centre = jnp.where(same, centre, 0.0).astype(BF16)
    side = jnp.where(gap == 0, -8.0, jnp.where(gap == 1, 2.0, 0.0))
    side = jnp.where(same, side, 0.0).astype(BF16)
    edge = 2 * modes
    to, frm = iotas((size, 2 * edge))
    row = jnp.where(frm < edge, frm // modes, rows - 4 + frm // modes)
    place = one_hot((frm % modes == to // rows) & (row == to % rows))
    for c in range(width // chunk):
        cols = pl.ds(c * chunk, chunk)
        terms = jnp.concatenate([above_ref[:, :, cols].reshape(edge, chunk), below_ref[:, :, cols].reshape(edge, chunk)], axis=0)
        operand = x_ref[:, :, cols].reshape(size, chunk)
        inner = STIFF * jnp.dot(centre, operand, preferred_element_type=F32) + jnp.dot(place, terms, preferred_element_type=F32)
        inner_ref[:, :, cols] = inner.reshape(modes, rows, chunk)
        side_ref[:, :, cols] = jnp.dot(side, operand, preferred_element_type=F32).reshape(modes, rows, chunk)
    lane = lax.broadcasted_iota(jnp.int32, (rows, width), 1)

    def one_mode(m, _):
        x = x_ref[m].astype(F32)
        y = side_ref[m]
        right = shifted(y + shifted(x, lane, 1), lane, 1)
        left = shifted(y + shifted(x, lane, -1), lane, -1)
        out_ref[m] = (inner_ref[m] + STIFF * (right + left)).astype(BF16)
        return 0

    lax.fori_loop(0, modes, one_mode, 0)


def stencil(x, above, below, field):
    modes, rows, width = x.shape
    edge = pl.BlockSpec((2, modes, width), lambda i: (0, field, 0))
    whole = pl.BlockSpec(x.shape, lambda i: (0, 0, 0))
    return pl.pallas_call(
        functools.partial(stencil_kernel, 512),
        grid=(1,),
        in_specs=[whole, edge, edge],
        out_specs=whole,
        out_shape=pltpu.HBM(x.shape, BF16),
        scratch_shapes=[pltpu.VMEM(x.shape, F32)] * 2,
        compiler_params=pltpu.CompilerParams(vmem_limit_bytes=VMEM),
        cost_estimate=pl.CostEstimate(flops=8589934592, bytes_accessed=4 * MIB, transcendentals=0),
        name="stencil",
    )(pltpu.with_memory_space_constraint(x, HBM), above, below)


def edges_kernel(chunk, disp_ref, dir_ref, low_ref, high_ref):
    modes, rows, width = disp_ref.shape
    last = rows - 1
    to, frm = iotas((4 * modes, modes * rows))
    part, row = to // modes, frm % rows
    same = to % modes == frm // rows
    outer = jnp.where(part < 2, 0, last)
    inner = jnp.where(part < 2, 1, last - 1)
    full = (part == 1) | (part == 2)
    plain = jnp.where(
        full,
        jnp.where(row == outer, -8.0, jnp.where(row == inner, 1.0, 0.0)),
        jnp.where(row == outer, 1.0, 0.0),
    )
    plain = jnp.where(same, plain, 0.0).astype(BF16)
    to, frm = iotas((2 * modes, modes * rows))
    outer = jnp.where(to // modes == 0, 0, last)
    corner = jnp.where((to % modes == frm // rows) & (frm % rows == outer), 2.0, 0.0).astype(BF16)
    lane = lax.broadcasted_iota(jnp.int32, (2 * modes, width), 1)
    for field, ref in enumerate((disp_ref, dir_ref)):
        at = pl.ds(field * modes, modes)
        x = ref[...].reshape(modes * rows, width)
        terms = jnp.dot(plain, x, preferred_element_type=F32)
        corners = jnp.dot(corner, x, preferred_element_type=F32)
        corners = shifted(corners, lane, 1) + shifted(corners, lane, -1)
        low_ref[0, at, :] = (STIFF * terms[:modes]).astype(BF16)
        low_ref[1, at, :] = (STIFF * (terms[modes : 2 * modes] + corners[:modes])).astype(BF16)
        high_ref[0, at, :] = (STIFF * (terms[2 * modes : 3 * modes] + corners[modes:])).astype(BF16)
        high_ref[1, at, :] = (STIFF * terms[3 * modes :]).astype(BF16)


def edges(displacement, direction):
    modes, rows, width = displacement.shape
    whole = pl.BlockSpec(displacement.shape, lambda i: (0, 0, 0))
    edge = pl.BlockSpec((2, 2 * modes, width), lambda i: (0, 0, 0))
    return pl.pallas_call(
        functools.partial(edges_kernel, 512),
        grid=(1,),
        in_specs=[whole, whole],
        out_specs=[edge, edge],
        out_shape=[pltpu.HBM((2, 2 * modes, width), BF16)] * 2,
        compiler_params=pltpu.CompilerParams(vmem_limit_bytes=VMEM),
        cost_estimate=pl.CostEstimate(flops=1048576, bytes_accessed=1048576, transcendentals=0),
        name="edges",
    )(pltpu.with_memory_space_constraint(displacement, HBM), pltpu.with_memory_space_constraint(direction, HBM))


def merge_kernel(groups, force_ref, res_ref, tan_ref, res_out, tan_out, in_buf, buf, in_sem, out_sem):
    count, rows, both, each = force_ref.shape
    modes = both // 2
    size = both * rows
    per = count // groups
    span = per * each

    def loads(g):
        cols = pl.ds(g * span, span)
        return [
            pltpu.make_async_copy(ref.at[:, :, cols], in_buf.at[f, :, :, cols], in_sem.at[f, g])
            for f, ref in enumerate((res_ref, tan_ref))
        ]

    def stores(g):
        cols = pl.ds(g * span, span)
        return [
            pltpu.make_async_copy(buf.at[f, :, :, cols], ref.at[:, :, cols], out_sem.at[f, g])
            for f, ref in enumerate((res_out, tan_out))
        ]

    for g in range(groups):
        for copy in loads(g):
            copy.start()
    to, frm = iotas((size, size))
    hit = (to % rows == frm // both) & (to // rows == frm % both)
    moves = jnp.where(hit, jnp.where(to // rows < modes, -1.0, 2.0), 0.0).astype(BF16)
    for g in range(groups):
        for copy in loads(g):
            copy.wait()
        for d in range(g * per, (g + 1) * per):
            cols = pl.ds(d * each, each)
            moved = jnp.dot(moves, force_ref[d].reshape(size, each), preferred_element_type=F32)
            moved = moved.reshape(2, modes, rows, each)
            buf[:, :, :, cols] = in_buf[:, :, :, cols].astype(F32) + moved
        for copy in stores(g):
            copy.start()
    for g in range(groups):
        for copy in stores(g):
            copy.wait()


def merge(force, res, tan, groups=8):
    count, rows, both, each = force.shape
    vmem = pl.BlockSpec(memory_space=pltpu.VMEM)
    hbm = pl.BlockSpec(memory_space=HBM)
    return pl.pallas_call(
        functools.partial(merge_kernel, groups),
        in_specs=[vmem, hbm, hbm],
        out_specs=[hbm] * 2,
        out_shape=[pltpu.HBM(res.shape, F32)] * 2,
        scratch_shapes=[
            pltpu.VMEM((2,) + res.shape, BF16),
            pltpu.VMEM((2,) + res.shape, F32),
            pltpu.SemaphoreType.DMA((2, groups)),
            pltpu.SemaphoreType.DMA((2, groups)),
        ],
        compiler_params=pltpu.CompilerParams(vmem_limit_bytes=VMEM),
        cost_estimate=pl.CostEstimate(flops=2 * (both * rows) ** 2 * each * count, bytes_accessed=10 * MIB, transcendentals=0),
        name="merge",
    )(force, pltpu.with_memory_space_constraint(res, HBM), pltpu.with_memory_space_constraint(tan, HBM))


def shards(displacement, direction, quad_nodes, quad_weights, gap_nominal, pressure_load, degrees):
    count = lax.axis_size("mode")
    bands = lax.axis_size("space")
    send = pack(displacement, direction, count)
    table = basis(quad_nodes, degrees)
    scale = quad_weights * pressure_load * (STEEP * STEEP)
    table_w = (table.astype(F32) * scale[None, :]).astype(BF16)
    table_t = -STEEP * table.T
    shift = jnp.broadcast_to((STEEP * (gap_nominal - FLOOR))[:, None], (gap_nominal.shape[0], 128))
    first, second, send = lax.optimization_barrier((displacement, direction, send))
    got = lax.all_to_all(send, "mode", split_axis=0, concat_axis=0, tiled=True)
    low, high = edges(first, second)
    above = lax.ppermute(high, "space", [(i, i + 1) for i in range(bands - 1)])
    below = lax.ppermute(low, "space", [(i + 1, i) for i in range(bands - 1)])
    got, _, _ = lax.optimization_barrier((got, low, high))
    force = quad_forces(got, table_t, table_w, shift)
    back = lax.all_to_all(force, "mode", split_axis=0, concat_axis=0, tiled=True)
    res = stencil(displacement, above, below, 0)
    tan = stencil(direction, above, below, 1)
    return tuple(merge(back, res, tan))


def solution(mesh):
    in_specs = (P("mode", "space", None), P("mode", "space", None), P(), P(), P(), P(), P())
    out_specs = (P("mode", "space", None), P("mode", "space", None))
    return jax.shard_map(shards, mesh=mesh, in_specs=in_specs, out_specs=out_specs, check_vma=False)
```

```python
import functools

import jax
import jax.numpy as jnp
from jax import lax
from jax.experimental import pallas as pl
from jax.experimental.pallas import tpu as pltpu
from jax.sharding import PartitionSpec as P

HALF_ROOT = 0.7071067811865476
THIRD_NORM = 0.4082482904638631
FOURTH_NORM = 0.2041241452319315
FLOOR = 0.3
STEEP = 4.0
STIFF = 0.1
LOG2E = 1.4426950408889634
LN2 = 0.6931471805599453
MIB = 1 << 20
VMEM = 24 * MIB
F32 = jnp.float32
BF16 = jnp.bfloat16
HBM = pltpu.HBM


def basis(quad_nodes, degrees):
    points = quad_nodes[None, :, :]
    degree_grid = degrees[:, None, :]
    square = points * points
    third = (square * points - 3.0 * points) * THIRD_NORM
    fourth = (square * square - 6.0 * square + 3.0) * FOURTH_NORM
    second = (square - 1.0) * HALF_ROOT
    factor = jnp.where(
        degree_grid == 0,
        1.0,
        jnp.where(
            degree_grid == 1,
            points,
            jnp.where(degree_grid == 2, second, jnp.where(degree_grid == 3, third, fourth)),
        ),
    )
    return jnp.prod(factor, axis=2).astype(BF16)


def iotas(shape):
    return lax.broadcasted_iota(jnp.int32, shape, 0), lax.broadcasted_iota(jnp.int32, shape, 1)


def one_hot(hit):
    return jnp.where(hit, 1.0, 0.0).astype(BF16)


def in_hbm(x):
    return pltpu.with_memory_space_constraint(x, HBM)


def shifted(v, lane, by):
    width = v.shape[-1]
    inside = lane < width - 1 if by > 0 else lane > 0
    return jnp.where(inside, pltpu.roll(v, width - 1 if by > 0 else 1, 1), 0.0)


def pack_kernel(groups, step, disp_ref, dir_ref, send_ref, in_buf, out_buf, in_sem, out_sem):
    modes, rows, width = disp_ref.shape
    count, _, both, each = send_ref.shape
    size = both * rows
    per = count // groups
    span = per * each

    def loads(g):
        cols = pl.ds(g * span, span)
        return [
            pltpu.make_async_copy(ref.at[:, :, cols], in_buf.at[f, :, :, cols], in_sem.at[f, g])
            for f, ref in enumerate((disp_ref, dir_ref))
        ]

    def store(g):
        at = pl.ds(g * per, per)
        return pltpu.make_async_copy(out_buf.at[at], send_ref.at[at], out_sem.at[g])

    for g in range(groups):
        for copy in loads(g):
            copy.start()
    to, frm = iotas((size, size))
    perm = one_hot(frm == (to % both) * rows + to // both)
    for g in range(groups):
        for copy in loads(g):
            copy.wait()
        for d in range(g * per, (g + 1) * per, step):
            fields = in_buf[:, :, :, pl.ds(d * each, step * each)].reshape(size, step * each)
            moved = jnp.dot(perm, fields, preferred_element_type=F32).astype(BF16)
            for k in range(step):
                out_buf[d + k] = moved[:, k * each : (k + 1) * each].reshape(rows, both, each)
        store(g).start()
    for g in range(groups):
        store(g).wait()


def pack(displacement, direction, count, groups=8, step=2):
    modes, rows, width = displacement.shape
    each = width // count
    both = 2 * modes
    hbm = pl.BlockSpec(memory_space=HBM)
    shape = (count, rows, both, each)
    return pl.pallas_call(
        functools.partial(pack_kernel, groups, step),
        in_specs=[hbm, hbm],
        out_specs=hbm,
        out_shape=pltpu.HBM(shape, BF16),
        scratch_shapes=[
            pltpu.VMEM((2, modes, rows, width), BF16),
            pltpu.VMEM(shape, BF16),
            pltpu.SemaphoreType.DMA((2, groups)),
            pltpu.SemaphoreType.DMA((groups,)),
        ],
        compiler_params=pltpu.CompilerParams(vmem_limit_bytes=VMEM),
        cost_estimate=pl.CostEstimate(flops=2 * (2 * modes * rows) ** 2 * width, bytes_accessed=4 * MIB, transcendentals=0),
        name="pack",
    )(in_hbm(displacement), in_hbm(direction))


def quad_kernel(chunk, deep, got_ref, table_t_ref, table_w_ref, shift_ref, out_ref, out_buf, w_ref, cross_ref, out_sem):
    count, rows, both, each = got_ref.shape
    per = count // 2
    modes = both // 2
    quad = table_t_ref.shape[0]
    total = per * modes
    pairs = rows // deep
    steps = 2 * pairs

    def store(i):
        at = pl.ds(i // pairs * per, per)
        lines = pl.ds(i % pairs * deep, deep)
        return pltpu.make_async_copy(out_buf.at[at, lines], out_ref.at[at, lines], out_sem.at[i])

    def field_rows(i, f):
        at = pl.ds(i // pairs * per, per)
        lines = [
            got_ref[at, i % pairs * deep + k, f * modes : (f + 1) * modes, :].reshape(total, each) for k in range(deep)
        ]
        return jnp.concatenate(lines, axis=1)

    frm, to = iotas((deep * each, deep * each))
    far = frm % each - to % each
    for band in range(2):
        near = frm // each == band
        full = to // each == 1 - band
        value = jnp.where(far == 0, jnp.where(near, jnp.where(full, -8.0, 1.0), jnp.where(full, 1.0, 0.0)), 0.0)
        cross_ref[band] = jnp.where((jnp.abs(far) == 1) & near & full, 2.0, value).astype(BF16)

    def one_step(i, _):
        disp = field_rows(i, 0)
        dire = field_rows(i, 1)
        for q in range(quad // chunk):
            at = pl.ds(q * chunk, chunk)
            left = table_t_ref[at, :]
            shift = shift_ref[at, :]
            shift = jnp.concatenate([shift] * (deep * each // shift.shape[1]), axis=1)
            s = shift + jnp.dot(left, disp, preferred_element_type=F32)
            probe = jnp.dot(left, dire, preferred_element_type=F32)
            e = jnp.exp2(jnp.minimum(s, 80.0) * LOG2E)
            one = 1.0 + e
            big = jnp.maximum(s, jnp.log2(one) * LN2) + STEEP * FLOOR
            inv = pl.reciprocal(big, approx=True)
            sig = e * pl.reciprocal(one, approx=True)
            square = inv * inv
            w_ref[0, at, :] = square.astype(BF16)
            w_ref[1, at, :] = ((sig * inv) * (square * probe)).astype(BF16)
        table_w = table_w_ref[...]
        weight = jnp.where((i == pairs - 1) | (i == pairs), STIFF, 0.0)
        for f, factor in enumerate((-1.0, 0.5)):
            cross = jnp.dot(field_rows(steps - 1 - i, f), cross_ref[i // pairs], preferred_element_type=F32)
            force = jnp.dot(table_w, w_ref[f], preferred_element_type=F32)
            force = (force + (factor * weight) * cross).astype(BF16)
            for k in range(deep):
                part = force[:, k * each : (k + 1) * each].reshape(per, modes, each)
                out_buf[pl.ds(i // pairs * per, per), i % pairs * deep + k, f * modes : (f + 1) * modes, :] = part
        store(i).start()
        return 0

    lax.fori_loop(0, steps, one_step, 0)
    for i in range(steps):
        store(i).wait()


def quad_forces(got, table_t, table_w, shift, deep=2):
    count, rows, both, each = got.shape
    quad, total = table_t.shape
    vmem = pl.BlockSpec(memory_space=pltpu.VMEM)
    return pl.pallas_call(
        functools.partial(quad_kernel, 128, deep),
        in_specs=[vmem] * 4,
        out_specs=pl.BlockSpec(memory_space=HBM),
        out_shape=pltpu.HBM(got.shape, BF16),
        scratch_shapes=[
            pltpu.VMEM(got.shape, BF16),
            pltpu.VMEM((2, quad, deep * each), BF16),
            pltpu.VMEM((2, deep * each, deep * each), BF16),
            pltpu.SemaphoreType.DMA((2 * rows // deep,)),
        ],
        compiler_params=pltpu.CompilerParams(vmem_limit_bytes=VMEM),
        cost_estimate=pl.CostEstimate(flops=1 << 10, bytes_accessed=1 << 10, transcendentals=0),
        name="quad_forces",
    )(got, table_t, table_w, shift)


def stencil_kernel(chunk, block, odd_ref, x_ref, outer_ref, ends_ref, out_ref, inner_ref, side_ref):
    modes, rows, width = x_ref.shape
    size = modes * rows
    blocks = width // block
    odd = odd_ref[0]
    to, frm = iotas((size, size + modes))
    gap = jnp.abs(to - frm)
    same = to // rows == frm // rows
    centre = jnp.where(gap == 0, 20.0, jnp.where(gap == 1, -8.0, jnp.where(gap == 2, 1.0, 0.0)))
    corner = (frm - size == to // rows) & (to % rows == (rows - 1) * (1 - odd))
    centre = jnp.where(frm < size, jnp.where(same, centre, 0.0), jnp.where(corner, 2.0, 0.0)).astype(BF16)
    to, frm = iotas((size, size))
    gap = jnp.abs(to - frm)
    side = jnp.where(gap == 0, -8.0, jnp.where(gap == 1, 2.0, 0.0))
    side = jnp.where(to // rows == frm // rows, side, 0.0).astype(BF16)
    to, frm = iotas((size, 2 * modes))
    place = one_hot((frm % modes == to // rows) & (to % rows == frm // modes + (rows - 2) * odd))
    item, col = iotas((ends_ref.shape[1], chunk))
    target = jnp.where(item < blocks, item * block - 1, (item - blocks + 1) * block)
    target = jnp.where(item < 2 * blocks, target, -1)
    for c in range(width // chunk):
        cols = pl.ds(c * chunk, chunk)
        x = x_ref[:, :, cols].reshape(size, chunk)
        spread = jnp.dot(ends_ref[...], one_hot(target == col + c * chunk), preferred_element_type=F32).astype(BF16)
        inner = jnp.dot(centre, jnp.concatenate([x, spread], axis=0), preferred_element_type=F32)
        terms = jnp.dot(place, outer_ref[:, :, cols].reshape(2 * modes, chunk), preferred_element_type=F32)
        inner_ref[:, :, cols] = (STIFF * inner + terms).reshape(modes, rows, chunk)
        side_ref[:, :, cols] = jnp.dot(side, x, preferred_element_type=F32).reshape(modes, rows, chunk)
    lane = lax.broadcasted_iota(jnp.int32, (rows, width), 1)

    def one_mode(m, _):
        x = x_ref[m].astype(F32)
        y = side_ref[m]
        right = shifted(y + shifted(x, lane, 1), lane, 1)
        left = shifted(y + shifted(x, lane, -1), lane, -1)
        out_ref[m] = (inner_ref[m] + STIFF * (right + left)).astype(BF16)
        return 0

    lax.fori_loop(0, modes, one_mode, 0)


def stencil(odd, x, outer, ends, field, count):
    modes, rows, width = x.shape
    whole = pl.BlockSpec((modes, rows, width), lambda i: (0, 0, 0))
    return pl.pallas_call(
        functools.partial(stencil_kernel, 512, width // count),
        grid=(1,),
        in_specs=[
            pl.BlockSpec(memory_space=pltpu.SMEM),
            whole,
            pl.BlockSpec((2, modes, width), lambda i: (0, field, 0)),
            pl.BlockSpec((modes, ends.shape[1]), lambda i: (field, 0)),
        ],
        out_specs=whole,
        out_shape=pltpu.HBM(x.shape, BF16),
        scratch_shapes=[pltpu.VMEM(x.shape, F32)] * 2,
        compiler_params=pltpu.CompilerParams(vmem_limit_bytes=VMEM),
        cost_estimate=pl.CostEstimate(flops=1 << 33, bytes_accessed=4 * MIB, transcendentals=0),
        name="stencil",
    )(odd, in_hbm(x), outer, ends)


def edges_kernel(block, odd_ref, disp_ref, dir_ref, terms_ref, ends_ref):
    modes, rows, width = disp_ref.shape
    size = modes * rows
    blocks = width // block
    odd = odd_ref[0]
    outer = (rows - 1) * odd
    inner = jnp.where(odd == 1, rows - 2, 1)
    to, frm = iotas((2 * modes, size))
    same = to % modes == frm // rows
    row = frm % rows
    full = to // modes == 1 - odd
    plain = jnp.where(row == outer, jnp.where(full, -8.0, 1.0), jnp.where(full & (row == inner), 1.0, 0.0))
    plain = jnp.where(same, plain, 0.0).astype(BF16)
    to, frm = iotas((modes, size))
    same = to == frm // rows
    corner = jnp.where(same & (frm % rows == outer), 2.0, 0.0).astype(BF16)
    facing = one_hot(same & (frm % rows == rows - 1 - outer))
    lane = lax.broadcasted_iota(jnp.int32, (modes, width), 1)
    col, item = iotas((width, ends_ref.shape[1]))
    source = jnp.where(item < blocks, item * block, (item - blocks) * block + block - 1)
    pick = one_hot((col == source) & (item < 2 * blocks))
    first = jnp.where(odd == 1, 1.0, 0.0)
    for f, ref in enumerate((disp_ref, dir_ref)):
        at = pl.ds(f * modes, modes)
        x = ref[...].reshape(size, width)
        terms = jnp.dot(plain, x, preferred_element_type=F32)
        corners = jnp.dot(corner, x, preferred_element_type=F32)
        corners = shifted(corners, lane, 1) + shifted(corners, lane, -1)
        terms_ref[0, at, :] = (STIFF * (terms[:modes] + first * corners)).astype(BF16)
        terms_ref[1, at, :] = (STIFF * (terms[modes:] + (1.0 - first) * corners)).astype(BF16)
        line = jnp.dot(facing, x, preferred_element_type=F32).astype(BF16)
        ends_ref[at, :] = jnp.dot(line, pick, preferred_element_type=F32).astype(BF16)


def edges(odd, displacement, direction, count):
    modes, rows, width = displacement.shape
    lanes = max(128, 2 * count)
    whole = pl.BlockSpec(displacement.shape, lambda i: (0, 0, 0))
    return pl.pallas_call(
        functools.partial(edges_kernel, width // count),
        grid=(1,),
        in_specs=[pl.BlockSpec(memory_space=pltpu.SMEM), whole, whole],
        out_specs=[
            pl.BlockSpec((2, 2 * modes, width), lambda i: (0, 0, 0)),
            pl.BlockSpec((2 * modes, lanes), lambda i: (0, 0)),
        ],
        out_shape=[pltpu.HBM((2, 2 * modes, width), BF16), pltpu.HBM((2 * modes, lanes), BF16)],
        compiler_params=pltpu.CompilerParams(vmem_limit_bytes=VMEM),
        cost_estimate=pl.CostEstimate(flops=1 << 20, bytes_accessed=1 << 20, transcendentals=0),
        name="edges",
    )(odd, in_hbm(displacement), in_hbm(direction))


def merge_kernel(groups, step, force_ref, res_ref, tan_ref, res_out, tan_out, in_buf, buf, in_sem, out_sem):
    count, rows, both, each = force_ref.shape
    modes = both // 2
    size = both * rows
    per = count // groups
    span = per * each

    def loads(g):
        cols = pl.ds(g * span, span)
        return [
            pltpu.make_async_copy(ref.at[:, :, cols], in_buf.at[f, :, :, cols], in_sem.at[f, g])
            for f, ref in enumerate((res_ref, tan_ref))
        ]

    def stores(g):
        cols = pl.ds(g * span, span)
        return [
            pltpu.make_async_copy(buf.at[f, :, :, cols], ref.at[:, :, cols], out_sem.at[f, g])
            for f, ref in enumerate((res_out, tan_out))
        ]

    for g in range(groups):
        for copy in loads(g):
            copy.start()
    to, frm = iotas((size, size))
    hit = (to % rows == frm // both) & (to // rows == frm % both)
    moves = jnp.where(hit, jnp.where(to // rows < modes, -1.0, 2.0), 0.0).astype(BF16)
    for g in range(groups):
        for copy in loads(g):
            copy.wait()
        for d in range(g * per, (g + 1) * per, step):
            cols = pl.ds(d * each, step * each)
            force = jnp.concatenate([force_ref[d + k].reshape(size, each) for k in range(step)], axis=1)
            moved = jnp.dot(moves, force, preferred_element_type=F32).reshape(2, modes, rows, step * each)
            buf[:, :, :, cols] = in_buf[:, :, :, cols].astype(F32) + moved
        for copy in stores(g):
            copy.start()
    for g in range(groups):
        for copy in stores(g):
            copy.wait()


def merge(force, res, tan, groups=8, step=2):
    count, rows, both, each = force.shape
    vmem = pl.BlockSpec(memory_space=pltpu.VMEM)
    hbm = pl.BlockSpec(memory_space=HBM)
    return pl.pallas_call(
        functools.partial(merge_kernel, groups, step),
        in_specs=[vmem, hbm, hbm],
        out_specs=[hbm] * 2,
        out_shape=[pltpu.HBM(res.shape, F32)] * 2,
        scratch_shapes=[
            pltpu.VMEM((2,) + res.shape, BF16),
            pltpu.VMEM((2,) + res.shape, F32),
            pltpu.SemaphoreType.DMA((2, groups)),
            pltpu.SemaphoreType.DMA((2, groups)),
        ],
        compiler_params=pltpu.CompilerParams(vmem_limit_bytes=VMEM),
        cost_estimate=pl.CostEstimate(flops=2 * (both * rows) ** 2 * each * count, bytes_accessed=10 * MIB, transcendentals=0),
        name="merge",
    )(force, in_hbm(res), in_hbm(tan))


def shards(displacement, direction, quad_nodes, quad_weights, gap_nominal, pressure_load, degrees):
    bands = lax.axis_size("space")
    count = 2 * lax.axis_size("mode")
    odd = (lax.axis_index("space") % 2).astype(jnp.int32).reshape(1)
    pairs = [[p * count + i for i in range(count)] for p in range(bands // 2)]

    def exchange(x):
        return lax.all_to_all(x, ("space", "mode"), split_axis=0, concat_axis=0, axis_index_groups=pairs, tiled=True)

    send = pack(displacement, direction, count)
    first, second, send = lax.optimization_barrier((displacement, direction, send))
    got = exchange(send)
    terms, ends = edges(odd, first, second, count)
    ends = lax.ppermute(ends, "space", [(i, i ^ 1) for i in range(bands)])
    terms, ends, got = lax.optimization_barrier((terms, ends, got))
    outer = lax.ppermute(terms, "space", [(i + a, i + b) for i in range(1, bands - 1, 2) for a, b in ((0, 1), (1, 0))])
    table = basis(quad_nodes, degrees)
    scale = quad_weights * pressure_load * (STEEP * STEEP)
    table_w = (table.astype(F32) * scale[None, :]).astype(BF16)
    table_t = -STEEP * table.T
    shift = jnp.broadcast_to((STEEP * (gap_nominal - FLOOR))[:, None], (gap_nominal.shape[0], 128))
    force = quad_forces(got, table_t, table_w, shift)
    back = exchange(force)
    res = stencil(odd, displacement, outer, ends, 0, count)
    tan = stencil(odd, direction, outer, ends, 1, count)
    return tuple(merge(back, res, tan))


def solution(mesh):
    in_specs = (P("mode", "space", None), P("mode", "space", None), P(), P(), P(), P(), P())
    out_specs = (P("mode", "space", None), P("mode", "space", None))
    return jax.shard_map(shards, mesh=mesh, in_specs=in_specs, out_specs=out_specs, check_vma=False)
```

```python
import functools

import jax
import jax.numpy as jnp
from jax import lax
from jax.experimental import pallas as pl
from jax.experimental.pallas import tpu as pltpu
from jax.sharding import PartitionSpec as P

HALF_ROOT = 0.7071067811865476
THIRD_NORM = 0.4082482904638631
FOURTH_NORM = 0.2041241452319315
FLOOR = 0.3
STEEP = 4.0
STIFF = 0.1
LOG2E = 1.4426950408889634
LN2 = 0.6931471805599453
MIB = 1 << 20
VMEM = 24 * MIB
F32 = jnp.float32
BF16 = jnp.bfloat16
HBM = pltpu.HBM


def basis(quad_nodes, degrees):
    points = quad_nodes[None, :, :]
    degree_grid = degrees[:, None, :]
    square = points * points
    third = (square * points - 3.0 * points) * THIRD_NORM
    fourth = (square * square - 6.0 * square + 3.0) * FOURTH_NORM
    second = (square - 1.0) * HALF_ROOT
    factor = jnp.where(
        degree_grid == 0,
        1.0,
        jnp.where(
            degree_grid == 1,
            points,
            jnp.where(degree_grid == 2, second, jnp.where(degree_grid == 3, third, fourth)),
        ),
    )
    return jnp.prod(factor, axis=2).astype(BF16)


def iotas(shape):
    return lax.broadcasted_iota(jnp.int32, shape, 0), lax.broadcasted_iota(jnp.int32, shape, 1)


def one_hot(hit):
    return jnp.where(hit, 1.0, 0.0).astype(BF16)


def in_hbm(x):
    return pltpu.with_memory_space_constraint(x, HBM)


def shifted(v, lane, by):
    width = v.shape[-1]
    inside = lane < width - 1 if by > 0 else lane > 0
    return jnp.where(inside, pltpu.roll(v, width - 1 if by > 0 else 1, 1), 0.0)


def pack_kernel(groups, early, step, disp_ref, dir_ref, send_ref, in_buf, out_buf, in_sem, out_sem):
    modes, rows, width = disp_ref.shape
    count, _, both, each = send_ref.shape
    size = both * rows
    per = count // groups
    span = per * each

    ahead = groups // early

    def loads(g):
        cols = pl.ds(g * ahead * span, ahead * span)
        return [
            pltpu.make_async_copy(ref.at[:, :, cols], in_buf.at[f, :, :, cols], in_sem.at[f, g])
            for f, ref in enumerate((disp_ref, dir_ref))
        ]

    def store(g):
        at = pl.ds(g * per, per)
        return pltpu.make_async_copy(out_buf.at[at], send_ref.at[at], out_sem.at[g])

    for g in range(early):
        for copy in loads(g):
            copy.start()
    to, frm = iotas((size, size))
    perm = one_hot(frm == (to % both) * rows + to // both)
    for g in range(groups):
        for copy in loads(g // ahead) if g % ahead == 0 else []:
            copy.wait()
        for d in range(g * per, (g + 1) * per, step):
            fields = in_buf[:, :, :, pl.ds(d * each, step * each)].reshape(size, step * each)
            moved = jnp.dot(perm, fields, preferred_element_type=F32).astype(BF16)
            for k in range(step):
                out_buf[d + k] = moved[:, k * each : (k + 1) * each].reshape(rows, both, each)
        store(g).start()
    for g in range(groups):
        store(g).wait()


def pack(displacement, direction, count, groups=4, early=2, step=2):
    modes, rows, width = displacement.shape
    each = width // count
    both = 2 * modes
    hbm = pl.BlockSpec(memory_space=HBM)
    shape = (count, rows, both, each)
    return pl.pallas_call(
        functools.partial(pack_kernel, groups, early, step),
        in_specs=[hbm, hbm],
        out_specs=hbm,
        out_shape=pltpu.HBM(shape, BF16),
        scratch_shapes=[
            pltpu.VMEM((2, modes, rows, width), BF16),
            pltpu.VMEM(shape, BF16),
            pltpu.SemaphoreType.DMA((2, early)),
            pltpu.SemaphoreType.DMA((groups,)),
        ],
        compiler_params=pltpu.CompilerParams(vmem_limit_bytes=VMEM),
        cost_estimate=pl.CostEstimate(flops=2 * (2 * modes * rows) ** 2 * width, bytes_accessed=4 * MIB, transcendentals=0),
        name="pack",
    )(in_hbm(displacement), in_hbm(direction))


def quad_kernel(chunk, deep, got_ref, table_t_ref, table_w_ref, shift_ref, out_ref, out_buf, w_ref, cross_ref, out_sem):
    count, rows, both, each = got_ref.shape
    per = count // 2
    modes = both // 2
    quad = table_t_ref.shape[0]
    total = per * modes
    pairs = rows // deep
    steps = 2 * pairs

    def store(i):
        at = pl.ds(i // pairs * per, per)
        lines = pl.ds(i % pairs * deep, deep)
        return pltpu.make_async_copy(out_buf.at[at, lines], out_ref.at[at, lines], out_sem.at[i])

    def field_rows(i, f):
        at = pl.ds(i // pairs * per, per)
        lines = [
            got_ref[at, i % pairs * deep + k, f * modes : (f + 1) * modes, :].reshape(total, each) for k in range(deep)
        ]
        return jnp.concatenate(lines, axis=1)

    frm, to = iotas((deep * each, deep * each))
    far = frm % each - to % each
    for band in range(2):
        near = frm // each == band
        full = to // each == 1 - band
        value = jnp.where(far == 0, jnp.where(near, jnp.where(full, -8.0, 1.0), jnp.where(full, 1.0, 0.0)), 0.0)
        cross_ref[band] = jnp.where((jnp.abs(far) == 1) & near & full, 2.0, value).astype(BF16)

    def forward(i):
        slot = i % 2
        disp = field_rows(i, 0)
        dire = field_rows(i, 1)
        for q in range(quad // chunk):
            at = pl.ds(q * chunk, chunk)
            left = table_t_ref[at, :]
            shift = shift_ref[at, :]
            shift = jnp.concatenate([shift] * (deep * each // shift.shape[1]), axis=1)
            s = shift + jnp.dot(left, disp, preferred_element_type=F32)
            probe = jnp.dot(left, dire, preferred_element_type=F32)
            e = jnp.exp2(jnp.minimum(s, 80.0) * LOG2E)
            one = 1.0 + e
            big = jnp.maximum(s, jnp.log2(one) * LN2) + STEEP * FLOOR
            inv = pl.reciprocal(big, approx=True)
            sig = e * pl.reciprocal(one, approx=True)
            square = inv * inv
            w_ref[slot, 0, at, :] = square.astype(BF16)
            w_ref[slot, 1, at, :] = ((sig * inv) * (square * probe)).astype(BF16)

    def back(i):
        band, pair = i // pairs, i % pairs
        for f, factor in enumerate((-STIFF, 0.5 * STIFF)):
            force = jnp.dot(table_w_ref[...], w_ref[i % 2, f], preferred_element_type=F32)
            if i in (pairs - 1, pairs):
                facing = field_rows(steps - 1 - i, f)
                force = force + factor * jnp.dot(facing, cross_ref[band], preferred_element_type=F32)
            force = force.astype(BF16)
            for k in range(deep):
                part = force[:, k * each : (k + 1) * each].reshape(per, modes, each)
                out_buf[band * per : (band + 1) * per, pair * deep + k, f * modes : (f + 1) * modes, :] = part
        store(i).start()

    for i in range(steps + 1):
        if i < steps:
            forward(i)
        if i > 0:
            back(i - 1)
    for i in range(steps):
        store(i).wait()


def quad_forces(got, table_t, table_w, shift, deep=2):
    count, rows, both, each = got.shape
    quad, total = table_t.shape
    vmem = pl.BlockSpec(memory_space=pltpu.VMEM)
    return pl.pallas_call(
        functools.partial(quad_kernel, 128, deep),
        in_specs=[vmem] * 4,
        out_specs=pl.BlockSpec(memory_space=HBM),
        out_shape=pltpu.HBM(got.shape, BF16),
        scratch_shapes=[
            pltpu.VMEM(got.shape, BF16),
            pltpu.VMEM((2, 2, quad, deep * each), BF16),
            pltpu.VMEM((2, deep * each, deep * each), BF16),
            pltpu.SemaphoreType.DMA((2 * rows // deep,)),
        ],
        compiler_params=pltpu.CompilerParams(vmem_limit_bytes=VMEM),
        cost_estimate=pl.CostEstimate(flops=1 << 10, bytes_accessed=1 << 10, transcendentals=0),
        name="quad_forces",
    )(got, table_t, table_w, shift)


def stencil_kernel(chunk, block, odd_ref, x_ref, outer_ref, ends_ref, out_ref, inner_ref, side_ref):
    modes, rows, width = x_ref.shape
    size = modes * rows
    blocks = width // block
    odd = odd_ref[0]
    to, frm = iotas((size, size + modes))
    gap = jnp.abs(to - frm)
    same = to // rows == frm // rows
    centre = jnp.where(gap == 0, 20.0, jnp.where(gap == 1, -8.0, jnp.where(gap == 2, 1.0, 0.0)))
    corner = (frm - size == to // rows) & (to % rows == (rows - 1) * (1 - odd))
    centre = jnp.where(frm < size, jnp.where(same, centre, 0.0), jnp.where(corner, 2.0, 0.0)).astype(BF16)
    to, frm = iotas((size, size))
    gap = jnp.abs(to - frm)
    side = jnp.where(gap == 0, -8.0, jnp.where(gap == 1, 2.0, 0.0))
    side = jnp.where(to // rows == frm // rows, side, 0.0).astype(BF16)
    to, frm = iotas((size, 2 * modes))
    place = one_hot((frm % modes == to // rows) & (to % rows == frm // modes + (rows - 2) * odd))
    item, col = iotas((ends_ref.shape[1], chunk))
    target = jnp.where(item < blocks, item * block - 1, (item - blocks + 1) * block)
    target = jnp.where(item < 2 * blocks, target, -1)
    for c in range(width // chunk):
        cols = pl.ds(c * chunk, chunk)
        x = x_ref[:, :, cols].reshape(size, chunk)
        spread = jnp.dot(ends_ref[...], one_hot(target == col + c * chunk), preferred_element_type=F32).astype(BF16)
        inner = jnp.dot(centre, jnp.concatenate([x, spread], axis=0), preferred_element_type=F32)
        terms = jnp.dot(place, outer_ref[:, :, cols].reshape(2 * modes, chunk), preferred_element_type=F32)
        inner_ref[:, :, cols] = (STIFF * inner + terms).reshape(modes, rows, chunk)
        side_ref[:, :, cols] = jnp.dot(side, x, preferred_element_type=F32).reshape(modes, rows, chunk)
    lane = lax.broadcasted_iota(jnp.int32, (rows, width), 1)

    def one_mode(m, _):
        x = x_ref[m].astype(F32)
        y = side_ref[m]
        right = shifted(y + shifted(x, lane, 1), lane, 1)
        left = shifted(y + shifted(x, lane, -1), lane, -1)
        out_ref[m] = (inner_ref[m] + STIFF * (right + left)).astype(BF16)
        return 0

    lax.fori_loop(0, modes, one_mode, 0)


def stencil(odd, x, outer, ends, field, count):
    modes, rows, width = x.shape
    whole = pl.BlockSpec((modes, rows, width), lambda i: (0, 0, 0))
    return pl.pallas_call(
        functools.partial(stencil_kernel, 512, width // count),
        grid=(1,),
        in_specs=[
            pl.BlockSpec(memory_space=pltpu.SMEM),
            whole,
            pl.BlockSpec((2, modes, width), lambda i: (0, field, 0)),
            pl.BlockSpec((modes, ends.shape[1]), lambda i: (field, 0)),
        ],
        out_specs=whole,
        out_shape=pltpu.HBM(x.shape, BF16),
        scratch_shapes=[pltpu.VMEM(x.shape, F32)] * 2,
        compiler_params=pltpu.CompilerParams(vmem_limit_bytes=VMEM),
        cost_estimate=pl.CostEstimate(flops=1 << 33, bytes_accessed=4 * MIB, transcendentals=0),
        name="stencil",
    )(odd, in_hbm(x), outer, ends)


def edges_kernel(block, odd_ref, disp_ref, dir_ref, terms_ref, ends_ref):
    modes, rows, width = disp_ref.shape
    size = modes * rows
    blocks = width // block
    odd = odd_ref[0]
    outer = (rows - 1) * odd
    inner = jnp.where(odd == 1, rows - 2, 1)
    to, frm = iotas((2 * modes, size))
    same = to % modes == frm // rows
    row = frm % rows
    full = to // modes == 1 - odd
    plain = jnp.where(row == outer, jnp.where(full, -8.0, 1.0), jnp.where(full & (row == inner), 1.0, 0.0))
    plain = jnp.where(same, plain, 0.0).astype(BF16)
    to, frm = iotas((modes, size))
    same = to == frm // rows
    corner = jnp.where(same & (frm % rows == outer), 2.0, 0.0).astype(BF16)
    facing = one_hot(same & (frm % rows == rows - 1 - outer))
    lane = lax.broadcasted_iota(jnp.int32, (modes, width), 1)
    col, item = iotas((width, ends_ref.shape[1]))
    source = jnp.where(item < blocks, item * block, (item - blocks) * block + block - 1)
    pick = one_hot((col == source) & (item < 2 * blocks))
    first = jnp.where(odd == 1, 1.0, 0.0)
    for f, ref in enumerate((disp_ref, dir_ref)):
        at = pl.ds(f * modes, modes)
        x = ref[...].reshape(size, width)
        terms = jnp.dot(plain, x, preferred_element_type=F32)
        corners = jnp.dot(corner, x, preferred_element_type=F32)
        corners = shifted(corners, lane, 1) + shifted(corners, lane, -1)
        terms_ref[0, at, :] = (STIFF * (terms[:modes] + first * corners)).astype(BF16)
        terms_ref[1, at, :] = (STIFF * (terms[modes:] + (1.0 - first) * corners)).astype(BF16)
        line = jnp.dot(facing, x, preferred_element_type=F32).astype(BF16)
        ends_ref[at, :] = jnp.dot(line, pick, preferred_element_type=F32).astype(BF16)


def edges(odd, displacement, direction, count):
    modes, rows, width = displacement.shape
    lanes = max(128, 2 * count)
    whole = pl.BlockSpec(displacement.shape, lambda i: (0, 0, 0))
    return pl.pallas_call(
        functools.partial(edges_kernel, width // count),
        grid=(1,),
        in_specs=[pl.BlockSpec(memory_space=pltpu.SMEM), whole, whole],
        out_specs=[
            pl.BlockSpec((2, 2 * modes, width), lambda i: (0, 0, 0)),
            pl.BlockSpec((2 * modes, lanes), lambda i: (0, 0)),
        ],
        out_shape=[pltpu.HBM((2, 2 * modes, width), BF16), pltpu.HBM((2 * modes, lanes), BF16)],
        compiler_params=pltpu.CompilerParams(vmem_limit_bytes=VMEM),
        cost_estimate=pl.CostEstimate(flops=1 << 20, bytes_accessed=1 << 20, transcendentals=0),
        name="edges",
    )(odd, in_hbm(displacement), in_hbm(direction))


def merge_kernel(groups, step, force_ref, res_ref, tan_ref, res_out, tan_out, in_buf, buf, in_sem, out_sem):
    count, rows, both, each = force_ref.shape
    modes = both // 2
    size = both * rows
    per = count // groups
    span = per * each

    def loads(g):
        cols = pl.ds(g * span, span)
        return [
            pltpu.make_async_copy(ref.at[:, :, cols], in_buf.at[f, :, :, cols], in_sem.at[f, g])
            for f, ref in enumerate((res_ref, tan_ref))
        ]

    def stores(g):
        cols = pl.ds(g * span, span)
        return [
            pltpu.make_async_copy(buf.at[f, :, :, cols], ref.at[:, :, cols], out_sem.at[f, g])
            for f, ref in enumerate((res_out, tan_out))
        ]

    for g in range(groups):
        for copy in loads(g):
            copy.start()
    to, frm = iotas((size, size))
    hit = (to % rows == frm // both) & (to // rows == frm % both)
    moves = jnp.where(hit, jnp.where(to // rows < modes, -1.0, 2.0), 0.0).astype(BF16)
    for g in range(groups):
        for copy in loads(g):
            copy.wait()
        for d in range(g * per, (g + 1) * per, step):
            cols = pl.ds(d * each, step * each)
            force = jnp.concatenate([force_ref[d + k].reshape(size, each) for k in range(step)], axis=1)
            moved = jnp.dot(moves, force, preferred_element_type=F32).reshape(2, modes, rows, step * each)
            buf[:, :, :, cols] = in_buf[:, :, :, cols].astype(F32) + moved
        for copy in stores(g):
            copy.start()
    for g in range(groups):
        for copy in stores(g):
            copy.wait()


def merge(force, res, tan, groups=4, step=2):
    count, rows, both, each = force.shape
    vmem = pl.BlockSpec(memory_space=pltpu.VMEM)
    hbm = pl.BlockSpec(memory_space=HBM)
    return pl.pallas_call(
        functools.partial(merge_kernel, groups, step),
        in_specs=[vmem, hbm, hbm],
        out_specs=[hbm] * 2,
        out_shape=[pltpu.HBM(res.shape, F32)] * 2,
        scratch_shapes=[
            pltpu.VMEM((2,) + res.shape, BF16),
            pltpu.VMEM((2,) + res.shape, F32),
            pltpu.SemaphoreType.DMA((2, groups)),
            pltpu.SemaphoreType.DMA((2, groups)),
        ],
        compiler_params=pltpu.CompilerParams(vmem_limit_bytes=VMEM),
        cost_estimate=pl.CostEstimate(flops=2 * (both * rows) ** 2 * each * count, bytes_accessed=10 * MIB, transcendentals=0),
        name="merge",
    )(force, in_hbm(res), in_hbm(tan))


def shards(displacement, direction, quad_nodes, quad_weights, gap_nominal, pressure_load, degrees):
    bands = lax.axis_size("space")
    count = 2 * lax.axis_size("mode")
    odd = (lax.axis_index("space") % 2).astype(jnp.int32).reshape(1)
    pairs = [[p * count + i for i in range(count)] for p in range(bands // 2)]

    def exchange(x):
        return lax.all_to_all(x, ("space", "mode"), split_axis=0, concat_axis=0, axis_index_groups=pairs, tiled=True)

    send = pack(displacement, direction, count)
    first, second, send = lax.optimization_barrier((displacement, direction, send))
    got = exchange(send)
    terms, ends = edges(odd, first, second, count)
    ends = lax.ppermute(ends, "space", [(i, i ^ 1) for i in range(bands)])
    terms, ends, got = lax.optimization_barrier((terms, ends, got))
    outer = lax.ppermute(terms, "space", [(i + a, i + b) for i in range(1, bands - 1, 2) for a, b in ((0, 1), (1, 0))])
    table = basis(quad_nodes, degrees)
    scale = quad_weights * pressure_load * (STEEP * STEEP)
    table_w = (table.astype(F32) * scale[None, :]).astype(BF16)
    table_t = -STEEP * table.T
    shift = jnp.broadcast_to((STEEP * (gap_nominal - FLOOR))[:, None], (gap_nominal.shape[0], 128))
    force = quad_forces(got, table_t, table_w, shift)
    back = exchange(force)
    res = stencil(odd, displacement, outer, ends, 0, count)
    tan = stencil(odd, direction, outer, ends, 1, count)
    return tuple(merge(back, res, tan))


def solution(mesh):
    in_specs = (P("mode", "space", None), P("mode", "space", None), P(), P(), P(), P(), P())
    out_specs = (P("mode", "space", None), P("mode", "space", None))
    return jax.shard_map(shards, mesh=mesh, in_specs=in_specs, out_specs=out_specs, check_vma=False)
```

```python
import functools

import jax
import jax.numpy as jnp
from jax import lax
from jax.experimental import pallas as pl
from jax.experimental.pallas import tpu as pltpu
from jax.sharding import PartitionSpec as P

HALF_ROOT = 0.7071067811865476
THIRD_NORM = 0.4082482904638631
FOURTH_NORM = 0.2041241452319315
FLOOR = 0.3
STEEP = 4.0
STIFF = 0.1
LOG2E = 1.4426950408889634
LN2 = 0.6931471805599453
MIB = 1 << 20
VMEM = 24 * MIB
F32 = jnp.float32
BF16 = jnp.bfloat16
HBM = pltpu.HBM


def basis(quad_nodes, degrees):
    points = quad_nodes[None, :, :]
    degree_grid = degrees[:, None, :]
    square = points * points
    third = (square * points - 3.0 * points) * THIRD_NORM
    fourth = (square * square - 6.0 * square + 3.0) * FOURTH_NORM
    second = (square - 1.0) * HALF_ROOT
    factor = jnp.where(
        degree_grid == 0,
        1.0,
        jnp.where(
            degree_grid == 1,
            points,
            jnp.where(degree_grid == 2, second, jnp.where(degree_grid == 3, third, fourth)),
        ),
    )
    return jnp.prod(factor, axis=2).astype(BF16)


def iotas(shape):
    return lax.broadcasted_iota(jnp.int32, shape, 0), lax.broadcasted_iota(jnp.int32, shape, 1)


def one_hot(hit):
    return jnp.where(hit, 1.0, 0.0).astype(BF16)


def in_hbm(x):
    return pltpu.with_memory_space_constraint(x, HBM)


def shifted(v, lane, by):
    width = v.shape[-1]
    inside = lane < width - 1 if by > 0 else lane > 0
    return jnp.where(inside, pltpu.roll(v, width - 1 if by > 0 else 1, 1), 0.0)


def pack_kernel(groups, early, step, disp_ref, dir_ref, send_ref, in_buf, out_buf, in_sem, out_sem):
    modes, rows, width = disp_ref.shape
    count, _, both, each = send_ref.shape
    size = both * rows
    per = count // groups
    span = per * each

    ahead = groups // early

    def loads(g):
        cols = pl.ds(g * ahead * span, ahead * span)
        return [
            pltpu.make_async_copy(ref.at[:, :, cols], in_buf.at[f, :, :, cols], in_sem.at[f, g])
            for f, ref in enumerate((disp_ref, dir_ref))
        ]

    def store(g):
        at = pl.ds(g * per, per)
        return pltpu.make_async_copy(out_buf.at[at], send_ref.at[at], out_sem.at[g])

    for g in range(early):
        for copy in loads(g):
            copy.start()
    to, frm = iotas((size, size))
    perm = one_hot(frm == (to % both) * rows + to // both)
    for g in range(groups):
        for copy in loads(g // ahead) if g % ahead == 0 else []:
            copy.wait()
        for d in range(g * per, (g + 1) * per, step):
            fields = in_buf[:, :, :, pl.ds(d * each, step * each)].reshape(size, step * each)
            moved = jnp.dot(perm, fields, preferred_element_type=F32).astype(BF16)
            for k in range(step):
                out_buf[d + k] = moved[:, k * each : (k + 1) * each].reshape(rows, both, each)
        store(g).start()
    for g in range(groups):
        store(g).wait()


def pack(displacement, direction, count, groups=4, early=2, step=2):
    modes, rows, width = displacement.shape
    each = width // count
    both = 2 * modes
    hbm = pl.BlockSpec(memory_space=HBM)
    shape = (count, rows, both, each)
    return pl.pallas_call(
        functools.partial(pack_kernel, groups, early, step),
        in_specs=[hbm, hbm],
        out_specs=hbm,
        out_shape=pltpu.HBM(shape, BF16),
        scratch_shapes=[
            pltpu.VMEM((2, modes, rows, width), BF16),
            pltpu.VMEM(shape, BF16),
            pltpu.SemaphoreType.DMA((2, early)),
            pltpu.SemaphoreType.DMA((groups,)),
        ],
        compiler_params=pltpu.CompilerParams(vmem_limit_bytes=VMEM),
        cost_estimate=pl.CostEstimate(flops=2 * (2 * modes * rows) ** 2 * width, bytes_accessed=4 * MIB, transcendentals=0),
        name="pack",
    )(in_hbm(displacement), in_hbm(direction))


def quad_kernel(chunk, deep, got_ref, table_t_ref, table_w_ref, shift_ref, out_ref, out_buf, w_ref, cross_ref, out_sem):
    count, rows, both, each = got_ref.shape
    per = count // 2
    modes = both // 2
    quad = table_t_ref.shape[0]
    total = per * modes
    pairs = rows // deep
    steps = 2 * pairs

    def store(i):
        at = pl.ds(i // pairs * per, per)
        lines = pl.ds(i % pairs * deep, deep)
        return pltpu.make_async_copy(out_buf.at[at, lines], out_ref.at[at, lines], out_sem.at[i])

    def field_rows(i, f):
        at = pl.ds(i // pairs * per, per)
        lines = [
            got_ref[at, i % pairs * deep + k, f * modes : (f + 1) * modes, :].reshape(total, each) for k in range(deep)
        ]
        return jnp.concatenate(lines, axis=1)

    frm, to = iotas((deep * each, deep * each))
    far = frm % each - to % each
    for band in range(2):
        near = frm // each == band
        full = to // each == 1 - band
        value = jnp.where(far == 0, jnp.where(near, jnp.where(full, -8.0, 1.0), jnp.where(full, 1.0, 0.0)), 0.0)
        cross_ref[band] = jnp.where((jnp.abs(far) == 1) & near & full, 2.0, value).astype(BF16)

    def forward(i):
        slot = i % 2
        disp = field_rows(i, 0)
        dire = field_rows(i, 1)
        for q in range(quad // chunk):
            at = pl.ds(q * chunk, chunk)
            left = table_t_ref[at, :]
            shift = shift_ref[at, :]
            shift = jnp.concatenate([shift] * (deep * each // shift.shape[1]), axis=1)
            s = shift + jnp.dot(left, disp, preferred_element_type=F32)
            probe = jnp.dot(left, dire, preferred_element_type=F32)
            e = jnp.exp2(jnp.minimum(s, 80.0) * LOG2E)
            one = 1.0 + e
            big = jnp.maximum(s, jnp.log2(one) * LN2) + STEEP * FLOOR
            inv = pl.reciprocal(big, approx=True)
            sig = e * pl.reciprocal(one, approx=True)
            square = inv * inv
            w_ref[slot, 0, at, :] = square.astype(BF16)
            w_ref[slot, 1, at, :] = ((sig * inv) * (square * probe)).astype(BF16)

    def back(i):
        band, pair = i // pairs, i % pairs
        for f, factor in enumerate((-STIFF, 0.5 * STIFF)):
            force = jnp.dot(table_w_ref[...], w_ref[i % 2, f], preferred_element_type=F32)
            if i in (pairs - 1, pairs):
                facing = field_rows(steps - 1 - i, f)
                force = force + factor * jnp.dot(facing, cross_ref[band], preferred_element_type=F32)
            force = force.astype(BF16)
            for k in range(deep):
                part = force[:, k * each : (k + 1) * each].reshape(per, modes, each)
                out_buf[band * per : (band + 1) * per, pair * deep + k, f * modes : (f + 1) * modes, :] = part
        store(i).start()

    for i in range(steps + 1):
        if i < steps:
            forward(i)
        if i > 0:
            back(i - 1)
    for i in range(steps):
        store(i).wait()


def quad_forces(got, table_t, table_w, shift, deep=2):
    count, rows, both, each = got.shape
    quad, total = table_t.shape
    vmem = pl.BlockSpec(memory_space=pltpu.VMEM)
    return pl.pallas_call(
        functools.partial(quad_kernel, 128, deep),
        in_specs=[vmem] * 4,
        out_specs=pl.BlockSpec(memory_space=HBM),
        out_shape=pltpu.HBM(got.shape, BF16),
        scratch_shapes=[
            pltpu.VMEM(got.shape, BF16),
            pltpu.VMEM((2, 2, quad, deep * each), BF16),
            pltpu.VMEM((2, deep * each, deep * each), BF16),
            pltpu.SemaphoreType.DMA((2 * rows // deep,)),
        ],
        compiler_params=pltpu.CompilerParams(vmem_limit_bytes=VMEM),
        cost_estimate=pl.CostEstimate(flops=3 << 31, bytes_accessed=1 << 10, transcendentals=0),
        name="quad_forces",
    )(got, table_t, table_w, shift)


def stencil_kernel(chunk, x_ref, out_ref, side_ref):
    modes, rows, width = x_ref.shape
    size = modes * rows
    to, frm = iotas((size, size))
    gap = jnp.abs(to - frm)
    same = to // rows == frm // rows
    centre = jnp.where(gap == 0, 20.0, jnp.where(gap == 1, -8.0, jnp.where(gap == 2, 1.0, 0.0)))
    centre = jnp.where(same, centre, 0.0).astype(BF16)
    side = jnp.where(gap == 0, -8.0, jnp.where(gap == 1, 2.0, 0.0))
    side = jnp.where(same, side, 0.0).astype(BF16)
    for c in range(width // chunk):
        cols = pl.ds(c * chunk, chunk)
        x = x_ref[:, :, cols].reshape(size, chunk)
        out_ref[:, :, cols] = jnp.dot(centre, x, preferred_element_type=F32).reshape(modes, rows, chunk)
        side_ref[:, :, cols] = jnp.dot(side, x, preferred_element_type=F32).reshape(modes, rows, chunk)
    lane = lax.broadcasted_iota(jnp.int32, (rows, width), 1)

    def one_mode(m, _):
        x = x_ref[m].astype(F32)
        y = side_ref[m]
        right = shifted(y + shifted(x, lane, 1), lane, 1)
        left = shifted(y + shifted(x, lane, -1), lane, -1)
        out_ref[m] = STIFF * (out_ref[m] + right + left)
        return 0

    lax.fori_loop(0, modes, one_mode, 0)


def stencil(x):
    whole = pl.BlockSpec(x.shape, lambda i: (0, 0, 0))
    return pl.pallas_call(
        functools.partial(stencil_kernel, 512),
        grid=(1,),
        in_specs=[whole],
        out_specs=whole,
        out_shape=pltpu.HBM(x.shape, F32),
        scratch_shapes=[pltpu.VMEM(x.shape, F32)],
        compiler_params=pltpu.CompilerParams(vmem_limit_bytes=VMEM),
        cost_estimate=pl.CostEstimate(flops=1 << 30, bytes_accessed=1 << 20, transcendentals=0),
        name="stencil",
    )(in_hbm(x))


def outer_kernel(block, blocks, odd_ref, outer_ref, ends_ref, res_ref, tan_ref, res_out, tan_out):
    modes, rows, chunk = res_ref.shape
    size = modes * rows
    odd = odd_ref[0]
    to, frm = iotas((size, modes))
    corner = one_hot((frm == to // rows) & (to % rows == (rows - 1) * (1 - odd)))
    item, col = iotas((ends_ref.shape[1], chunk))
    target = jnp.where(item < blocks, item * block - 1, (item - blocks + 1) * block)
    target = jnp.where(item < 2 * blocks, target, -1)
    spread = jnp.dot(ends_ref[...], one_hot(target == col + pl.program_id(0) * chunk), preferred_element_type=F32).astype(BF16)
    to, frm = iotas((size, 2 * modes))
    place = one_hot((frm % modes == to // rows) & (to % rows == frm // modes + (rows - 2) * odd))
    for f, (ref, out) in enumerate(((res_ref, res_out), (tan_ref, tan_out))):
        terms = outer_ref[:, f * modes : (f + 1) * modes, :].reshape(2 * modes, chunk)
        terms = jnp.dot(place, terms, preferred_element_type=F32)
        corners = jnp.dot(corner, spread[f * modes : (f + 1) * modes], preferred_element_type=F32)
        terms = (terms + (2.0 * STIFF) * corners).reshape(modes, rows, chunk)
        out[...] = (ref[...] + terms).astype(BF16)


def add_outer(odd, outer, ends, res, tan, count, steps=4):
    modes, rows, width = res.shape
    field = pl.BlockSpec((modes, rows, width // steps), lambda i: (0, 0, i))
    return pl.pallas_call(
        functools.partial(outer_kernel, width // count, count),
        grid=(steps,),
        in_specs=[
            pl.BlockSpec(memory_space=pltpu.SMEM),
            pl.BlockSpec((2, 2 * modes, width // steps), lambda i: (0, 0, i)),
            pl.BlockSpec(ends.shape, lambda i: (0, 0)),
            field,
            field,
        ],
        out_specs=[field, field],
        out_shape=[pltpu.HBM(res.shape, BF16)] * 2,
        compiler_params=pltpu.CompilerParams(vmem_limit_bytes=VMEM),
        cost_estimate=pl.CostEstimate(flops=5 << 32, bytes_accessed=7 * MIB, transcendentals=0),
        name="add_outer",
    )(odd, outer, ends, in_hbm(res), in_hbm(tan))


def edges_kernel(block, odd_ref, disp_ref, dir_ref, terms_ref, ends_ref):
    modes, rows, width = disp_ref.shape
    size = modes * rows
    blocks = width // block
    odd = odd_ref[0]
    outer = (rows - 1) * odd
    inner = jnp.where(odd == 1, rows - 2, 1)
    to, frm = iotas((2 * modes, size))
    same = to % modes == frm // rows
    row = frm % rows
    full = to // modes == 1 - odd
    plain = jnp.where(row == outer, jnp.where(full, -8.0, 1.0), jnp.where(full & (row == inner), 1.0, 0.0))
    plain = jnp.where(same, plain, 0.0).astype(BF16)
    to, frm = iotas((modes, size))
    same = to == frm // rows
    corner = jnp.where(same & (frm % rows == outer), 2.0, 0.0).astype(BF16)
    facing = one_hot(same & (frm % rows == rows - 1 - outer))
    lane = lax.broadcasted_iota(jnp.int32, (modes, width), 1)
    col, item = iotas((width, ends_ref.shape[1]))
    source = jnp.where(item < blocks, item * block, (item - blocks) * block + block - 1)
    pick = one_hot((col == source) & (item < 2 * blocks))
    first = jnp.where(odd == 1, 1.0, 0.0)
    for f, ref in enumerate((disp_ref, dir_ref)):
        at = pl.ds(f * modes, modes)
        x = ref[...].reshape(size, width)
        terms = jnp.dot(plain, x, preferred_element_type=F32)
        corners = jnp.dot(corner, x, preferred_element_type=F32)
        corners = shifted(corners, lane, 1) + shifted(corners, lane, -1)
        terms_ref[0, at, :] = (STIFF * (terms[:modes] + first * corners)).astype(BF16)
        terms_ref[1, at, :] = (STIFF * (terms[modes:] + (1.0 - first) * corners)).astype(BF16)
        line = jnp.dot(facing, x, preferred_element_type=F32).astype(BF16)
        ends_ref[at, :] = jnp.dot(line, pick, preferred_element_type=F32).astype(BF16)


def edges(odd, displacement, direction, count):
    modes, rows, width = displacement.shape
    lanes = max(128, 2 * count)
    whole = pl.BlockSpec(displacement.shape, lambda i: (0, 0, 0))
    return pl.pallas_call(
        functools.partial(edges_kernel, width // count),
        grid=(1,),
        in_specs=[pl.BlockSpec(memory_space=pltpu.SMEM), whole, whole],
        out_specs=[
            pl.BlockSpec((2, 2 * modes, width), lambda i: (0, 0, 0)),
            pl.BlockSpec((2 * modes, lanes), lambda i: (0, 0)),
        ],
        out_shape=[pltpu.HBM((2, 2 * modes, width), BF16), pltpu.HBM((2 * modes, lanes), BF16)],
        compiler_params=pltpu.CompilerParams(vmem_limit_bytes=VMEM),
        cost_estimate=pl.CostEstimate(flops=1 << 20, bytes_accessed=1 << 20, transcendentals=0),
        name="edges",
    )(odd, in_hbm(displacement), in_hbm(direction))


def merge_kernel(groups, step, force_ref, res_ref, tan_ref, res_out, tan_out, in_buf, buf, in_sem, out_sem):
    count, rows, both, each = force_ref.shape
    modes = both // 2
    size = both * rows
    per = count // groups
    span = per * each

    def loads(g):
        cols = pl.ds(g * span, span)
        return [
            pltpu.make_async_copy(ref.at[:, :, cols], in_buf.at[f, :, :, cols], in_sem.at[f, g])
            for f, ref in enumerate((res_ref, tan_ref))
        ]

    def stores(g):
        cols = pl.ds(g * span, span)
        return [
            pltpu.make_async_copy(buf.at[f, :, :, cols], ref.at[:, :, cols], out_sem.at[f, g])
            for f, ref in enumerate((res_out, tan_out))
        ]

    for g in range(groups):
        for copy in loads(g):
            copy.start()
    to, frm = iotas((size, size))
    hit = (to % rows == frm // both) & (to // rows == frm % both)
    moves = jnp.where(hit, jnp.where(to // rows < modes, -1.0, 2.0), 0.0).astype(BF16)
    for g in range(groups):
        for copy in loads(g):
            copy.wait()
        for d in range(g * per, (g + 1) * per, step):
            cols = pl.ds(d * each, step * each)
            force = jnp.concatenate([force_ref[d + k].reshape(size, each) for k in range(step)], axis=1)
            moved = jnp.dot(moves, force, preferred_element_type=F32).reshape(2, modes, rows, step * each)
            buf[:, :, :, cols] = in_buf[:, :, :, cols].astype(F32) + moved
        for copy in stores(g):
            copy.start()
    for g in range(groups):
        for copy in stores(g):
            copy.wait()


def merge(force, res, tan, groups=4, step=2):
    count, rows, both, each = force.shape
    vmem = pl.BlockSpec(memory_space=pltpu.VMEM)
    hbm = pl.BlockSpec(memory_space=HBM)
    return pl.pallas_call(
        functools.partial(merge_kernel, groups, step),
        in_specs=[vmem, hbm, hbm],
        out_specs=[hbm] * 2,
        out_shape=[pltpu.HBM(res.shape, F32)] * 2,
        scratch_shapes=[
            pltpu.VMEM((2,) + res.shape, BF16),
            pltpu.VMEM((2,) + res.shape, F32),
            pltpu.SemaphoreType.DMA((2, groups)),
            pltpu.SemaphoreType.DMA((2, groups)),
        ],
        compiler_params=pltpu.CompilerParams(vmem_limit_bytes=VMEM),
        cost_estimate=pl.CostEstimate(flops=2 * (both * rows) ** 2 * each * count, bytes_accessed=10 * MIB, transcendentals=0),
        name="merge",
    )(force, in_hbm(res), in_hbm(tan))


def shards(displacement, direction, quad_nodes, quad_weights, gap_nominal, pressure_load, degrees):
    bands = lax.axis_size("space")
    count = 2 * lax.axis_size("mode")
    odd = (lax.axis_index("space") % 2).astype(jnp.int32).reshape(1)
    pairs = [[p * count + i for i in range(count)] for p in range(bands // 2)]

    def exchange(x):
        return lax.all_to_all(x, ("space", "mode"), split_axis=0, concat_axis=0, axis_index_groups=pairs, tiled=True)

    send = pack(displacement, direction, count)
    first, second, send = lax.optimization_barrier((displacement, direction, send))
    got = exchange(send)
    terms, ends = edges(odd, first, second, count)
    ends = lax.ppermute(ends, "space", [(i, i ^ 1) for i in range(bands)])
    res, tan = stencil(first), stencil(second)
    table = basis(quad_nodes, degrees)
    scale = quad_weights * pressure_load * (STEEP * STEEP)
    table_w = (table.astype(F32) * scale[None, :]).astype(BF16)
    table_t = -STEEP * table.T
    shift = jnp.broadcast_to((STEEP * (gap_nominal - FLOOR))[:, None], (gap_nominal.shape[0], 128))
    terms, res, tan, table_t, table_w, shift = lax.optimization_barrier((terms, res, tan, table_t, table_w, shift))
    outer = lax.ppermute(terms, "space", [(i + a, i + b) for i in range(1, bands - 1, 2) for a, b in ((0, 1), (1, 0))])
    got, ends = lax.optimization_barrier((got, ends))
    force = quad_forces(got, table_t, table_w, shift)
    back = exchange(force)
    res, tan = add_outer(odd, outer, ends, res, tan, count)
    return tuple(merge(back, res, tan))


def solution(mesh):
    in_specs = (P("mode", "space", None), P("mode", "space", None), P(), P(), P(), P(), P())
    out_specs = (P("mode", "space", None), P("mode", "space", None))
    return jax.shard_map(shards, mesh=mesh, in_specs=in_specs, out_specs=out_specs, check_vma=False)
```

```python
import functools

import jax
import jax.numpy as jnp
from jax import lax
from jax.experimental import pallas as pl
from jax.experimental.pallas import tpu as pltpu
from jax.sharding import PartitionSpec as P

HALF_ROOT = 0.7071067811865476
THIRD_NORM = 0.4082482904638631
FOURTH_NORM = 0.2041241452319315
FLOOR = 0.3
STEEP = 4.0
STIFF = 0.1
LOG2E = 1.4426950408889634
LN2 = 0.6931471805599453
MIB = 1 << 20
VMEM = 24 * MIB
F32 = jnp.float32
BF16 = jnp.bfloat16
HBM = pltpu.HBM


def basis(quad_nodes, degrees):
    points = quad_nodes[None, :, :]
    degree_grid = degrees[:, None, :]
    square = points * points
    third = (square * points - 3.0 * points) * THIRD_NORM
    fourth = (square * square - 6.0 * square + 3.0) * FOURTH_NORM
    second = (square - 1.0) * HALF_ROOT
    factor = jnp.where(
        degree_grid == 0,
        1.0,
        jnp.where(
            degree_grid == 1,
            points,
            jnp.where(degree_grid == 2, second, jnp.where(degree_grid == 3, third, fourth)),
        ),
    )
    return jnp.prod(factor, axis=2).astype(BF16)


def iotas(shape):
    return lax.broadcasted_iota(jnp.int32, shape, 0), lax.broadcasted_iota(jnp.int32, shape, 1)


def one_hot(hit):
    return jnp.where(hit, 1.0, 0.0).astype(BF16)


def in_hbm(x):
    return pltpu.with_memory_space_constraint(x, HBM)


def shifted(v, lane, by):
    width = v.shape[-1]
    inside = lane < width - 1 if by > 0 else lane > 0
    return jnp.where(inside, pltpu.roll(v, width - 1 if by > 0 else 1, 1), 0.0)


def pack_kernel(groups, early, step, disp_ref, dir_ref, send_ref, in_buf, out_buf, in_sem, out_sem):
    modes, rows, width = disp_ref.shape
    count, _, both, each = send_ref.shape
    size = both * rows
    per = count // groups
    span = per * each

    ahead = groups // early

    def loads(g):
        cols = pl.ds(g * ahead * span, ahead * span)
        return [
            pltpu.make_async_copy(ref.at[:, :, cols], in_buf.at[f, :, :, cols], in_sem.at[f, g])
            for f, ref in enumerate((disp_ref, dir_ref))
        ]

    def store(g):
        at = pl.ds(g * per, per)
        return pltpu.make_async_copy(out_buf.at[at], send_ref.at[at], out_sem.at[g])

    for g in range(early):
        for copy in loads(g):
            copy.start()
    to, frm = iotas((size, size))
    perm = one_hot(frm == (to % both) * rows + to // both)
    for g in range(groups):
        for copy in loads(g // ahead) if g % ahead == 0 else []:
            copy.wait()
        for d in range(g * per, (g + 1) * per, step):
            fields = in_buf[:, :, :, pl.ds(d * each, step * each)].reshape(size, step * each)
            moved = jnp.dot(perm, fields, preferred_element_type=F32).astype(BF16)
            for k in range(step):
                out_buf[d + k] = moved[:, k * each : (k + 1) * each].reshape(rows, both, each)
        store(g).start()
    for g in range(groups):
        store(g).wait()


def pack(displacement, direction, count, groups=4, early=2, step=2):
    modes, rows, width = displacement.shape
    each = width // count
    both = 2 * modes
    hbm = pl.BlockSpec(memory_space=HBM)
    shape = (count, rows, both, each)
    return pl.pallas_call(
        functools.partial(pack_kernel, groups, early, step),
        in_specs=[hbm, hbm],
        out_specs=hbm,
        out_shape=pltpu.HBM(shape, BF16),
        scratch_shapes=[
            pltpu.VMEM((2, modes, rows, width), BF16),
            pltpu.VMEM(shape, BF16),
            pltpu.SemaphoreType.DMA((2, early)),
            pltpu.SemaphoreType.DMA((groups,)),
        ],
        compiler_params=pltpu.CompilerParams(vmem_limit_bytes=VMEM),
        cost_estimate=pl.CostEstimate(flops=2 * (2 * modes * rows) ** 2 * width, bytes_accessed=4 * MIB, transcendentals=0),
        name="pack",
    )(in_hbm(displacement), in_hbm(direction))


def quad_kernel(chunk, deep, got_ref, table_t_ref, table_w_ref, shift_ref, out_ref, out_buf, w_ref, cross_ref, out_sem):
    count, rows, both, each = got_ref.shape
    per = count // 2
    modes = both // 2
    quad = table_t_ref.shape[0]
    total = per * modes
    pairs = rows // deep
    steps = 2 * pairs

    def store(i):
        at = pl.ds(i // pairs * per, per)
        lines = pl.ds(i % pairs * deep, deep)
        return pltpu.make_async_copy(out_buf.at[at, lines], out_ref.at[at, lines], out_sem.at[i])

    def field_rows(i, f):
        at = pl.ds(i // pairs * per, per)
        lines = [
            got_ref[at, i % pairs * deep + k, f * modes : (f + 1) * modes, :].reshape(total, each) for k in range(deep)
        ]
        return jnp.concatenate(lines, axis=1)

    frm, to = iotas((deep * each, deep * each))
    far = frm % each - to % each
    for band in range(2):
        near = frm // each == band
        full = to // each == 1 - band
        value = jnp.where(far == 0, jnp.where(near, jnp.where(full, -8.0, 1.0), jnp.where(full, 1.0, 0.0)), 0.0)
        cross_ref[band] = jnp.where((jnp.abs(far) == 1) & near & full, 2.0, value).astype(BF16)

    def forward(i):
        slot = i % 2
        disp = field_rows(i, 0)
        dire = field_rows(i, 1)
        for q in range(quad // chunk):
            at = pl.ds(q * chunk, chunk)
            left = table_t_ref[at, :]
            shift = shift_ref[at, :]
            shift = jnp.concatenate([shift] * (deep * each // shift.shape[1]), axis=1)
            s = shift + jnp.dot(left, disp, preferred_element_type=F32)
            probe = jnp.dot(left, dire, preferred_element_type=F32)
            e = jnp.exp2(jnp.minimum(s, 80.0) * LOG2E)
            one = 1.0 + e
            big = jnp.maximum(s, jnp.log2(one) * LN2) + STEEP * FLOOR
            inv = pl.reciprocal(big, approx=True)
            sig = e * pl.reciprocal(one, approx=True)
            square = inv * inv
            w_ref[slot, 0, at, :] = square.astype(BF16)
            w_ref[slot, 1, at, :] = ((sig * inv) * (square * probe)).astype(BF16)

    def back(i):
        band, pair = i // pairs, i % pairs
        for f, factor in enumerate((-STIFF, 0.5 * STIFF)):
            force = jnp.dot(table_w_ref[...], w_ref[i % 2, f], preferred_element_type=F32)
            if i in (pairs - 1, pairs):
                facing = field_rows(steps - 1 - i, f)
                force = force + factor * jnp.dot(facing, cross_ref[band], preferred_element_type=F32)
            force = force.astype(BF16)
            for k in range(deep):
                part = force[:, k * each : (k + 1) * each].reshape(per, modes, each)
                out_buf[band * per : (band + 1) * per, pair * deep + k, f * modes : (f + 1) * modes, :] = part
        store(i).start()

    for i in range(steps + 1):
        if i < steps:
            forward(i)
        if i > 0:
            back(i - 1)
    for i in range(steps):
        store(i).wait()


def quad_forces(got, table_t, table_w, shift, deep=2):
    count, rows, both, each = got.shape
    quad, total = table_t.shape
    vmem = pl.BlockSpec(memory_space=pltpu.VMEM)
    return pl.pallas_call(
        functools.partial(quad_kernel, 128, deep),
        in_specs=[vmem] * 4,
        out_specs=pl.BlockSpec(memory_space=HBM),
        out_shape=pltpu.HBM(got.shape, BF16),
        scratch_shapes=[
            pltpu.VMEM(got.shape, BF16),
            pltpu.VMEM((2, 2, quad, deep * each), BF16),
            pltpu.VMEM((2, deep * each, deep * each), BF16),
            pltpu.SemaphoreType.DMA((2 * rows // deep,)),
        ],
        compiler_params=pltpu.CompilerParams(vmem_limit_bytes=VMEM),
        cost_estimate=pl.CostEstimate(flops=3 << 31, bytes_accessed=1 << 10, transcendentals=0),
        name="quad_forces",
    )(got, table_t, table_w, shift)


def stencil_kernel(chunk, x_ref, out_ref, side_ref):
    modes, rows, width = x_ref.shape
    size = modes * rows
    to, frm = iotas((size, size))
    gap = jnp.abs(to - frm)
    same = to // rows == frm // rows
    centre = jnp.where(gap == 0, 20.0, jnp.where(gap == 1, -8.0, jnp.where(gap == 2, 1.0, 0.0)))
    centre = jnp.where(same, centre, 0.0).astype(BF16)
    side = jnp.where(gap == 0, -8.0, jnp.where(gap == 1, 2.0, 0.0))
    side = jnp.where(same, side, 0.0).astype(BF16)
    for c in range(width // chunk):
        cols = pl.ds(c * chunk, chunk)
        x = x_ref[:, :, cols].reshape(size, chunk)
        out_ref[:, :, cols] = jnp.dot(centre, x, preferred_element_type=F32).reshape(modes, rows, chunk)
        side_ref[:, :, cols] = jnp.dot(side, x, preferred_element_type=F32).reshape(modes, rows, chunk)
    lane = lax.broadcasted_iota(jnp.int32, (rows, width), 1)

    def one_mode(m, _):
        x = x_ref[m].astype(F32)
        y = side_ref[m]
        right = shifted(y + shifted(x, lane, 1), lane, 1)
        left = shifted(y + shifted(x, lane, -1), lane, -1)
        out_ref[m] = STIFF * (out_ref[m] + right + left)
        return 0

    lax.fori_loop(0, modes, one_mode, 0)


def stencil(x):
    whole = pl.BlockSpec(x.shape, lambda i: (0, 0, 0))
    return pl.pallas_call(
        functools.partial(stencil_kernel, 512),
        grid=(1,),
        in_specs=[whole],
        out_specs=whole,
        out_shape=pltpu.HBM(x.shape, F32),
        scratch_shapes=[pltpu.VMEM(x.shape, F32)],
        compiler_params=pltpu.CompilerParams(vmem_limit_bytes=VMEM),
        cost_estimate=pl.CostEstimate(flops=1 << 30, bytes_accessed=1 << 20, transcendentals=0),
        name="stencil",
    )(in_hbm(x))


def outer_kernel(block, blocks, odd_ref, outer_ref, ends_ref, res_ref, tan_ref, res_out, tan_out):
    modes, rows, chunk = res_ref.shape
    size = modes * rows
    odd = odd_ref[0]
    to, frm = iotas((size, modes))
    corner = one_hot((frm == to // rows) & (to % rows == (rows - 1) * (1 - odd)))
    item, col = iotas((ends_ref.shape[1], chunk))
    target = jnp.where(item < blocks, item * block - 1, (item - blocks + 1) * block)
    target = jnp.where(item < 2 * blocks, target, -1)
    spread = jnp.dot(ends_ref[...], one_hot(target == col + pl.program_id(0) * chunk), preferred_element_type=F32).astype(BF16)
    to, frm = iotas((size, 2 * modes))
    place = one_hot((frm % modes == to // rows) & (to % rows == frm // modes + (rows - 2) * odd))
    for f, (ref, out) in enumerate(((res_ref, res_out), (tan_ref, tan_out))):
        terms = outer_ref[:, f * modes : (f + 1) * modes, :].reshape(2 * modes, chunk)
        terms = jnp.dot(place, terms, preferred_element_type=F32)
        corners = jnp.dot(corner, spread[f * modes : (f + 1) * modes], preferred_element_type=F32)
        terms = (terms + (2.0 * STIFF) * corners).reshape(modes, rows, chunk)
        out[...] = (ref[...] + terms).astype(BF16)


def add_outer(odd, outer, ends, res, tan, count, steps=4):
    modes, rows, width = res.shape
    field = pl.BlockSpec((modes, rows, width // steps), lambda i: (0, 0, i))
    return pl.pallas_call(
        functools.partial(outer_kernel, width // count, count),
        grid=(steps,),
        in_specs=[
            pl.BlockSpec(memory_space=pltpu.SMEM),
            pl.BlockSpec((2, 2 * modes, width // steps), lambda i: (0, 0, i)),
            pl.BlockSpec(ends.shape, lambda i: (0, 0)),
            field,
            field,
        ],
        out_specs=[field, field],
        out_shape=[pltpu.HBM(res.shape, BF16)] * 2,
        compiler_params=pltpu.CompilerParams(vmem_limit_bytes=VMEM),
        cost_estimate=pl.CostEstimate(flops=5 << 32, bytes_accessed=7 * MIB, transcendentals=0),
        name="add_outer",
    )(odd, outer, ends, in_hbm(res), in_hbm(tan))


def edges_kernel(block, odd_ref, disp_ref, dir_ref, terms_ref, ends_ref):
    modes, rows, width = disp_ref.shape
    size = modes * rows
    blocks = width // block
    odd = odd_ref[0]
    outer = (rows - 1) * odd
    inner = jnp.where(odd == 1, rows - 2, 1)
    to, frm = iotas((2 * modes, size))
    same = to % modes == frm // rows
    row = frm % rows
    full = to // modes == 1 - odd
    plain = jnp.where(row == outer, jnp.where(full, -8.0, 1.0), jnp.where(full & (row == inner), 1.0, 0.0))
    plain = jnp.where(same, plain, 0.0).astype(BF16)
    to, frm = iotas((modes, size))
    same = to == frm // rows
    corner = jnp.where(same & (frm % rows == outer), 2.0, 0.0).astype(BF16)
    facing = one_hot(same & (frm % rows == rows - 1 - outer))
    lane = lax.broadcasted_iota(jnp.int32, (modes, width), 1)
    col, item = iotas((width, ends_ref.shape[1]))
    source = jnp.where(item < blocks, item * block, (item - blocks) * block + block - 1)
    pick = one_hot((col == source) & (item < 2 * blocks))
    first = jnp.where(odd == 1, 1.0, 0.0)
    for f, ref in enumerate((disp_ref, dir_ref)):
        at = pl.ds(f * modes, modes)
        x = ref[...].reshape(size, width)
        terms = jnp.dot(plain, x, preferred_element_type=F32)
        corners = jnp.dot(corner, x, preferred_element_type=F32)
        corners = shifted(corners, lane, 1) + shifted(corners, lane, -1)
        terms_ref[0, at, :] = (STIFF * (terms[:modes] + first * corners)).astype(BF16)
        terms_ref[1, at, :] = (STIFF * (terms[modes:] + (1.0 - first) * corners)).astype(BF16)
        line = jnp.dot(facing, x, preferred_element_type=F32).astype(BF16)
        ends_ref[at, :] = jnp.dot(line, pick, preferred_element_type=F32).astype(BF16)


def edges(odd, displacement, direction, count):
    modes, rows, width = displacement.shape
    lanes = max(128, 2 * count)
    whole = pl.BlockSpec(displacement.shape, lambda i: (0, 0, 0))
    return pl.pallas_call(
        functools.partial(edges_kernel, width // count),
        grid=(1,),
        in_specs=[pl.BlockSpec(memory_space=pltpu.SMEM), whole, whole],
        out_specs=[
            pl.BlockSpec((2, 2 * modes, width), lambda i: (0, 0, 0)),
            pl.BlockSpec((2 * modes, lanes), lambda i: (0, 0)),
        ],
        out_shape=[pltpu.HBM((2, 2 * modes, width), BF16), pltpu.HBM((2 * modes, lanes), BF16)],
        compiler_params=pltpu.CompilerParams(vmem_limit_bytes=VMEM),
        cost_estimate=pl.CostEstimate(flops=1 << 20, bytes_accessed=1 << 20, transcendentals=0),
        name="edges",
    )(odd, in_hbm(displacement), in_hbm(direction))


def merge_kernel(groups, step, force_ref, res_ref, tan_ref, res_out, tan_out, in_buf, buf, in_sem, out_sem):
    count, rows, both, each = force_ref.shape
    modes = both // 2
    size = both * rows
    per = count // groups
    span = per * each

    def loads(g):
        cols = pl.ds(g * span, span)
        return [
            pltpu.make_async_copy(ref.at[:, :, cols], in_buf.at[f, :, :, cols], in_sem.at[f, g])
            for f, ref in enumerate((res_ref, tan_ref))
        ]

    def stores(g):
        cols = pl.ds(g * span, span)
        return [
            pltpu.make_async_copy(buf.at[f, :, :, cols], ref.at[:, :, cols], out_sem.at[f, g])
            for f, ref in enumerate((res_out, tan_out))
        ]

    for g in range(groups):
        for copy in loads(g):
            copy.start()
    to, frm = iotas((size, size))
    hit = (to % rows == frm // both) & (to // rows == frm % both)
    moves = jnp.where(hit, jnp.where(to // rows < modes, -1.0, 2.0), 0.0).astype(BF16)
    for g in range(groups):
        for copy in loads(g):
            copy.wait()
        for d in range(g * per, (g + 1) * per, step):
            cols = pl.ds(d * each, step * each)
            force = jnp.concatenate([force_ref[d + k].reshape(size, each) for k in range(step)], axis=1)
            moved = jnp.dot(moves, force, preferred_element_type=F32).reshape(2, modes, rows, step * each)
            buf[:, :, :, cols] = in_buf[:, :, :, cols].astype(F32) + moved
        for copy in stores(g):
            copy.start()
    for g in range(groups):
        for copy in stores(g):
            copy.wait()


def merge(force, res, tan, groups=4, step=2):
    count, rows, both, each = force.shape
    vmem = pl.BlockSpec(memory_space=pltpu.VMEM)
    hbm = pl.BlockSpec(memory_space=HBM)
    return pl.pallas_call(
        functools.partial(merge_kernel, groups, step),
        in_specs=[vmem, hbm, hbm],
        out_specs=[hbm] * 2,
        out_shape=[pltpu.HBM(res.shape, F32)] * 2,
        scratch_shapes=[
            pltpu.VMEM((2,) + res.shape, BF16),
            pltpu.VMEM((2,) + res.shape, F32),
            pltpu.SemaphoreType.DMA((2, groups)),
            pltpu.SemaphoreType.DMA((2, groups)),
        ],
        compiler_params=pltpu.CompilerParams(vmem_limit_bytes=VMEM),
        cost_estimate=pl.CostEstimate(flops=2 * (both * rows) ** 2 * each * count, bytes_accessed=10 * MIB, transcendentals=0),
        name="merge",
    )(force, in_hbm(res), in_hbm(tan))


def shards(displacement, direction, quad_nodes, quad_weights, gap_nominal, pressure_load, degrees):
    bands = lax.axis_size("space")
    count = 2 * lax.axis_size("mode")
    odd = (lax.axis_index("space") % 2).astype(jnp.int32).reshape(1)
    pairs = [[p * count + i for i in range(count)] for p in range(bands // 2)]

    def exchange(x):
        return lax.all_to_all(x, ("space", "mode"), split_axis=0, concat_axis=0, axis_index_groups=pairs, tiled=True)

    send = pack(displacement, direction, count)
    first, second, send = lax.optimization_barrier((displacement, direction, send))
    got = exchange(send)
    terms, ends = edges(odd, first, second, count)
    ends = lax.ppermute(ends, "space", [(i, i ^ 1) for i in range(bands)])
    res, tan = stencil(first), stencil(second)
    table = basis(quad_nodes, degrees)
    scale = quad_weights * pressure_load * (STEEP * STEEP)
    table_w = (table.astype(F32) * scale[None, :]).astype(BF16)
    turn = one_hot(jnp.equal(*iotas((table.shape[0],) * 2))) * (-STEEP)
    table_t = lax.dot_general(table, turn.astype(BF16), (((0,), (0,)), ((), ())), preferred_element_type=F32).astype(BF16)
    shift = jnp.broadcast_to((STEEP * (gap_nominal - FLOOR))[:, None], (gap_nominal.shape[0], 128))
    terms, res, tan, table_t, table_w, shift = lax.optimization_barrier((terms, res, tan, table_t, table_w, shift))
    outer = lax.ppermute(terms, "space", [(i + a, i + b) for i in range(1, bands - 1, 2) for a, b in ((0, 1), (1, 0))])
    got, ends = lax.optimization_barrier((got, ends))
    force = quad_forces(got, table_t, table_w, shift)
    back = exchange(force)
    res, tan = add_outer(odd, outer, ends, res, tan, count)
    return tuple(merge(back, res, tan))


def solution(mesh):
    in_specs = (P("mode", "space", None), P("mode", "space", None), P(), P(), P(), P(), P())
    out_specs = (P("mode", "space", None), P("mode", "space", None))
    return jax.shard_map(shards, mesh=mesh, in_specs=in_specs, out_specs=out_specs, check_vma=False)
```

```python
import functools

import jax
import jax.numpy as jnp
from jax import lax
from jax.experimental import pallas as pl
from jax.experimental.pallas import tpu as pltpu
from jax.sharding import PartitionSpec as P

HALF_ROOT = 0.7071067811865476
THIRD_NORM = 0.4082482904638631
FOURTH_NORM = 0.2041241452319315
FLOOR = 0.3
STEEP = 4.0
STIFF = 0.1
LOG2E = 1.4426950408889634
LN2 = 0.6931471805599453
MIB = 1 << 20
VMEM = 24 * MIB
F32 = jnp.float32
BF16 = jnp.bfloat16
HBM = pltpu.HBM


def basis(quad_nodes, degrees):
    points = quad_nodes[None, :, :]
    degree_grid = degrees[:, None, :]
    square = points * points
    third = (square * points - 3.0 * points) * THIRD_NORM
    fourth = (square * square - 6.0 * square + 3.0) * FOURTH_NORM
    second = (square - 1.0) * HALF_ROOT
    factor = jnp.where(
        degree_grid == 0,
        1.0,
        jnp.where(
            degree_grid == 1,
            points,
            jnp.where(degree_grid == 2, second, jnp.where(degree_grid == 3, third, fourth)),
        ),
    )
    return jnp.prod(factor, axis=2).astype(BF16)


def iotas(shape):
    return lax.broadcasted_iota(jnp.int32, shape, 0), lax.broadcasted_iota(jnp.int32, shape, 1)


def one_hot(hit):
    return jnp.where(hit, 1.0, 0.0).astype(BF16)


def in_hbm(x):
    return pltpu.with_memory_space_constraint(x, HBM)


def shifted(v, lane, by):
    width = v.shape[-1]
    inside = lane < width - 1 if by > 0 else lane > 0
    return jnp.where(inside, pltpu.roll(v, width - 1 if by > 0 else 1, 1), 0.0)


def pack_kernel(groups, early, step, disp_ref, dir_ref, send_ref, in_buf, out_buf, in_sem, out_sem):
    modes, rows, width = disp_ref.shape
    count, _, both, each = send_ref.shape
    size = both * rows
    per = count // groups
    span = per * each

    ahead = groups // early

    def loads(g):
        cols = pl.ds(g * ahead * span, ahead * span)
        return [
            pltpu.make_async_copy(ref.at[:, :, cols], in_buf.at[f, :, :, cols], in_sem.at[f, g])
            for f, ref in enumerate((disp_ref, dir_ref))
        ]

    def store(g):
        at = pl.ds(g * per, per)
        return pltpu.make_async_copy(out_buf.at[at], send_ref.at[at], out_sem.at[g])

    for g in range(early):
        for copy in loads(g):
            copy.start()
    to, frm = iotas((size, size))
    perm = one_hot(frm == (to % both) * rows + to // both)
    for g in range(groups):
        for copy in loads(g // ahead) if g % ahead == 0 else []:
            copy.wait()
        for d in range(g * per, (g + 1) * per, step):
            fields = in_buf[:, :, :, pl.ds(d * each, step * each)].reshape(size, step * each)
            moved = jnp.dot(perm, fields, preferred_element_type=F32).astype(BF16)
            for k in range(step):
                out_buf[d + k] = moved[:, k * each : (k + 1) * each].reshape(rows, both, each)
        store(g).start()
    for g in range(groups):
        store(g).wait()


def pack(displacement, direction, count, groups=4, early=2, step=2):
    modes, rows, width = displacement.shape
    each = width // count
    both = 2 * modes
    hbm = pl.BlockSpec(memory_space=HBM)
    shape = (count, rows, both, each)
    return pl.pallas_call(
        functools.partial(pack_kernel, groups, early, step),
        in_specs=[hbm, hbm],
        out_specs=hbm,
        out_shape=pltpu.HBM(shape, BF16),
        scratch_shapes=[
            pltpu.VMEM((2, modes, rows, width), BF16),
            pltpu.VMEM(shape, BF16),
            pltpu.SemaphoreType.DMA((2, early)),
            pltpu.SemaphoreType.DMA((groups,)),
        ],
        compiler_params=pltpu.CompilerParams(vmem_limit_bytes=VMEM),
        cost_estimate=pl.CostEstimate(flops=2 * (2 * modes * rows) ** 2 * width, bytes_accessed=4 * MIB, transcendentals=0),
        name="pack",
    )(in_hbm(displacement), in_hbm(direction))


def quad_kernel(chunk, deep, got_ref, table_t_ref, table_w_ref, shift_ref, out_ref, out_buf, w_ref, cross_ref, out_sem):
    count, rows, both, each = got_ref.shape
    per = count // 2
    modes = both // 2
    quad = table_t_ref.shape[0]
    total = per * modes
    pairs = rows // deep
    steps = 2 * pairs

    def store(i):
        at = pl.ds(i // pairs * per, per)
        lines = pl.ds(i % pairs * deep, deep)
        return pltpu.make_async_copy(out_buf.at[at, lines], out_ref.at[at, lines], out_sem.at[i])

    def field_rows(i, f):
        at = pl.ds(i // pairs * per, per)
        lines = [
            got_ref[at, i % pairs * deep + k, f * modes : (f + 1) * modes, :].reshape(total, each) for k in range(deep)
        ]
        return jnp.concatenate(lines, axis=1)

    frm, to = iotas((deep * each, deep * each))
    far = frm % each - to % each
    for band in range(2):
        near = frm // each == band
        full = to // each == 1 - band
        value = jnp.where(far == 0, jnp.where(near, jnp.where(full, -8.0, 1.0), jnp.where(full, 1.0, 0.0)), 0.0)
        cross_ref[band] = jnp.where((jnp.abs(far) == 1) & near & full, 2.0, value).astype(BF16)

    def forward(i):
        slot = i % 2
        disp = field_rows(i, 0)
        dire = field_rows(i, 1)
        for q in range(quad // chunk):
            at = pl.ds(q * chunk, chunk)
            left = table_t_ref[at, :]
            shift = shift_ref[at, :]
            shift = jnp.concatenate([shift] * (deep * each // shift.shape[1]), axis=1)
            s = shift + jnp.dot(left, disp, preferred_element_type=F32)
            probe = jnp.dot(left, dire, preferred_element_type=F32)
            e = jnp.exp2(jnp.minimum(s, 80.0) * LOG2E)
            one = 1.0 + e
            big = jnp.maximum(s, jnp.log2(one) * LN2) + STEEP * FLOOR
            inv = pl.reciprocal(big, approx=True)
            sig = e * pl.reciprocal(one, approx=True)
            square = inv * inv
            w_ref[slot, 0, at, :] = square.astype(BF16)
            w_ref[slot, 1, at, :] = ((sig * inv) * (square * probe)).astype(BF16)

    def back(i):
        band, pair = i // pairs, i % pairs
        for f, factor in enumerate((-STIFF, 0.5 * STIFF)):
            force = jnp.dot(table_w_ref[...], w_ref[i % 2, f], preferred_element_type=F32)
            if i in (pairs - 1, pairs):
                facing = field_rows(steps - 1 - i, f)
                force = force + factor * jnp.dot(facing, cross_ref[band], preferred_element_type=F32)
            force = force.astype(BF16)
            for k in range(deep):
                part = force[:, k * each : (k + 1) * each].reshape(per, modes, each)
                out_buf[band * per : (band + 1) * per, pair * deep + k, f * modes : (f + 1) * modes, :] = part
        store(i).start()

    for i in range(steps + 1):
        if i < steps:
            forward(i)
        if i > 0:
            back(i - 1)
    for i in range(steps):
        store(i).wait()


def quad_forces(got, table_t, table_w, shift, deep=2):
    count, rows, both, each = got.shape
    quad, total = table_t.shape
    vmem = pl.BlockSpec(memory_space=pltpu.VMEM)
    return pl.pallas_call(
        functools.partial(quad_kernel, 128, deep),
        in_specs=[vmem] * 4,
        out_specs=pl.BlockSpec(memory_space=HBM),
        out_shape=pltpu.HBM(got.shape, BF16),
        scratch_shapes=[
            pltpu.VMEM(got.shape, BF16),
            pltpu.VMEM((2, 2, quad, deep * each), BF16),
            pltpu.VMEM((2, deep * each, deep * each), BF16),
            pltpu.SemaphoreType.DMA((2 * rows // deep,)),
        ],
        compiler_params=pltpu.CompilerParams(vmem_limit_bytes=VMEM),
        cost_estimate=pl.CostEstimate(flops=3 << 31, bytes_accessed=1 << 10, transcendentals=0),
        name="quad_forces",
    )(got, table_t, table_w, shift)


def stencil_kernel(chunk, x_ref, out_ref, inner_ref, side_ref):
    modes, rows, width = x_ref.shape
    size = modes * rows
    to, frm = iotas((size, size))
    gap = jnp.abs(to - frm)
    same = to // rows == frm // rows
    centre = jnp.where(gap == 0, 20.0, jnp.where(gap == 1, -8.0, jnp.where(gap == 2, 1.0, 0.0)))
    centre = jnp.where(same, centre, 0.0).astype(BF16)
    side = jnp.where(gap == 0, -8.0, jnp.where(gap == 1, 2.0, 0.0))
    side = jnp.where(same, side, 0.0).astype(BF16)
    for c in range(width // chunk):
        cols = pl.ds(c * chunk, chunk)
        x = x_ref[:, :, cols].reshape(size, chunk)
        inner_ref[:, :, cols] = jnp.dot(centre, x, preferred_element_type=F32).reshape(modes, rows, chunk)
        side_ref[:, :, cols] = jnp.dot(side, x, preferred_element_type=F32).reshape(modes, rows, chunk)
    lane = lax.broadcasted_iota(jnp.int32, (rows, width), 1)

    def one_mode(m, _):
        x = x_ref[m].astype(F32)
        y = side_ref[m]
        right = shifted(y + shifted(x, lane, 1), lane, 1)
        left = shifted(y + shifted(x, lane, -1), lane, -1)
        out_ref[m] = (STIFF * (inner_ref[m] + right + left)).astype(BF16)
        return 0

    lax.fori_loop(0, modes, one_mode, 0)


def stencil(x):
    whole = pl.BlockSpec(x.shape, lambda i: (0, 0, 0))
    return pl.pallas_call(
        functools.partial(stencil_kernel, 512),
        grid=(1,),
        in_specs=[whole],
        out_specs=whole,
        out_shape=pltpu.HBM(x.shape, BF16),
        scratch_shapes=[pltpu.VMEM(x.shape, F32)] * 2,
        compiler_params=pltpu.CompilerParams(vmem_limit_bytes=VMEM),
        cost_estimate=pl.CostEstimate(flops=1 << 30, bytes_accessed=1 << 20, transcendentals=0),
        name="stencil",
    )(in_hbm(x))


def outer_kernel(block, blocks, odd_ref, outer_ref, ends_ref, res_ref, tan_ref, res_out, tan_out):
    modes, rows, chunk = res_ref.shape
    size = modes * rows
    odd = odd_ref[0]
    to, frm = iotas((size, modes))
    corner = one_hot((frm == to // rows) & (to % rows == (rows - 1) * (1 - odd)))
    item, col = iotas((ends_ref.shape[1], chunk))
    target = jnp.where(item < blocks, item * block - 1, (item - blocks + 1) * block)
    target = jnp.where(item < 2 * blocks, target, -1)
    spread = jnp.dot(ends_ref[...], one_hot(target == col + pl.program_id(0) * chunk), preferred_element_type=F32).astype(BF16)
    to, frm = iotas((size, 2 * modes))
    place = one_hot((frm % modes == to // rows) & (to % rows == frm // modes + (rows - 2) * odd))
    for f, (ref, out) in enumerate(((res_ref, res_out), (tan_ref, tan_out))):
        terms = outer_ref[:, f * modes : (f + 1) * modes, :].reshape(2 * modes, chunk)
        terms = jnp.dot(place, terms, preferred_element_type=F32)
        corners = jnp.dot(corner, spread[f * modes : (f + 1) * modes], preferred_element_type=F32)
        terms = (terms + (2.0 * STIFF) * corners).reshape(modes, rows, chunk)
        out[...] = (ref[...].astype(F32) + terms).astype(BF16)


def add_outer(odd, outer, ends, res, tan, count, steps=4):
    modes, rows, width = res.shape
    field = pl.BlockSpec((modes, rows, width // steps), lambda i: (0, 0, i))
    return pl.pallas_call(
        functools.partial(outer_kernel, width // count, count),
        grid=(steps,),
        in_specs=[
            pl.BlockSpec(memory_space=pltpu.SMEM),
            pl.BlockSpec((2, 2 * modes, width // steps), lambda i: (0, 0, i)),
            pl.BlockSpec(ends.shape, lambda i: (0, 0)),
            field,
            field,
        ],
        out_specs=[field, field],
        out_shape=[pltpu.HBM(res.shape, BF16)] * 2,
        compiler_params=pltpu.CompilerParams(vmem_limit_bytes=VMEM),
        cost_estimate=pl.CostEstimate(flops=5 << 32, bytes_accessed=7 * MIB, transcendentals=0),
        name="add_outer",
    )(odd, outer, ends, in_hbm(res), in_hbm(tan))


def edges_kernel(block, odd_ref, disp_ref, dir_ref, terms_ref, ends_ref):
    modes, rows, width = disp_ref.shape
    size = modes * rows
    blocks = width // block
    odd = odd_ref[0]
    outer = (rows - 1) * odd
    inner = jnp.where(odd == 1, rows - 2, 1)
    to, frm = iotas((2 * modes, size))
    same = to % modes == frm // rows
    row = frm % rows
    full = to // modes == 1 - odd
    plain = jnp.where(row == outer, jnp.where(full, -8.0, 1.0), jnp.where(full & (row == inner), 1.0, 0.0))
    plain = jnp.where(same, plain, 0.0).astype(BF16)
    to, frm = iotas((modes, size))
    same = to == frm // rows
    corner = jnp.where(same & (frm % rows == outer), 2.0, 0.0).astype(BF16)
    facing = one_hot(same & (frm % rows == rows - 1 - outer))
    lane = lax.broadcasted_iota(jnp.int32, (modes, width), 1)
    col, item = iotas((width, ends_ref.shape[1]))
    source = jnp.where(item < blocks, item * block, (item - blocks) * block + block - 1)
    pick = one_hot((col == source) & (item < 2 * blocks))
    first = jnp.where(odd == 1, 1.0, 0.0)
    for f, ref in enumerate((disp_ref, dir_ref)):
        at = pl.ds(f * modes, modes)
        x = ref[...].reshape(size, width)
        terms = jnp.dot(plain, x, preferred_element_type=F32)
        corners = jnp.dot(corner, x, preferred_element_type=F32)
        corners = shifted(corners, lane, 1) + shifted(corners, lane, -1)
        terms_ref[0, at, :] = (STIFF * (terms[:modes] + first * corners)).astype(BF16)
        terms_ref[1, at, :] = (STIFF * (terms[modes:] + (1.0 - first) * corners)).astype(BF16)
        line = jnp.dot(facing, x, preferred_element_type=F32).astype(BF16)
        ends_ref[at, :] = jnp.dot(line, pick, preferred_element_type=F32).astype(BF16)


def edges(odd, displacement, direction, count):
    modes, rows, width = displacement.shape
    lanes = max(128, 2 * count)
    whole = pl.BlockSpec(displacement.shape, lambda i: (0, 0, 0))
    return pl.pallas_call(
        functools.partial(edges_kernel, width // count),
        grid=(1,),
        in_specs=[pl.BlockSpec(memory_space=pltpu.SMEM), whole, whole],
        out_specs=[
            pl.BlockSpec((2, 2 * modes, width), lambda i: (0, 0, 0)),
            pl.BlockSpec((2 * modes, lanes), lambda i: (0, 0)),
        ],
        out_shape=[pltpu.HBM((2, 2 * modes, width), BF16), pltpu.HBM((2 * modes, lanes), BF16)],
        compiler_params=pltpu.CompilerParams(vmem_limit_bytes=VMEM),
        cost_estimate=pl.CostEstimate(flops=1 << 20, bytes_accessed=1 << 20, transcendentals=0),
        name="edges",
    )(odd, in_hbm(displacement), in_hbm(direction))


def merge_kernel(cuts, step, force_ref, res_ref, tan_ref, res_out, tan_out, in_buf, buf, in_sem, out_sem):
    count, rows, both, each = force_ref.shape
    modes = both // 2
    size = both * rows
    groups = len(cuts) - 1
    span = step * each

    def loads(g):
        cols = pl.ds(cuts[g] * span, (cuts[g + 1] - cuts[g]) * span)
        return [
            pltpu.make_async_copy(ref.at[:, :, cols], in_buf.at[f, :, :, cols], in_sem.at[f, g])
            for f, ref in enumerate((res_ref, tan_ref))
        ]

    def stores(g):
        cols = pl.ds(cuts[g] * span, (cuts[g + 1] - cuts[g]) * span)
        return [
            pltpu.make_async_copy(buf.at[f, :, :, cols], ref.at[:, :, cols], out_sem.at[f, g])
            for f, ref in enumerate((res_out, tan_out))
        ]

    for g in range(groups):
        for copy in loads(g):
            copy.start()
    to, frm = iotas((size, size))
    hit = (to % rows == frm // both) & (to // rows == frm % both)
    moves = jnp.where(hit, jnp.where(to // rows < modes, -1.0, 2.0), 0.0).astype(BF16)
    def moved(t):
        force = [force_ref[t * step + k].reshape(size, each) for k in range(step)]
        terms = jnp.dot(moves, jnp.concatenate(force, axis=1), preferred_element_type=F32)
        return terms.reshape(2, modes, rows, span)

    for t in range(cuts[1]):
        buf[:, :, :, pl.ds(t * span, span)] = moved(t)
    for g in range(groups):
        for copy in loads(g):
            copy.wait()
        for t in range(cuts[g], cuts[g + 1]):
            cols = pl.ds(t * span, span)
            terms = buf[:, :, :, cols] if g == 0 else moved(t)
            buf[:, :, :, cols] = in_buf[:, :, :, cols].astype(F32) + terms
        for copy in stores(g):
            copy.start()
    for g in range(groups):
        for copy in stores(g):
            copy.wait()


def merge(force, res, tan, cuts=(0, 4, 8, 12, 16), step=2):
    count, rows, both, each = force.shape
    vmem = pl.BlockSpec(memory_space=pltpu.VMEM)
    hbm = pl.BlockSpec(memory_space=HBM)
    return pl.pallas_call(
        functools.partial(merge_kernel, cuts, step),
        in_specs=[vmem, hbm, hbm],
        out_specs=[hbm] * 2,
        out_shape=[pltpu.HBM(res.shape, F32)] * 2,
        scratch_shapes=[
            pltpu.VMEM((2,) + res.shape, BF16),
            pltpu.VMEM((2,) + res.shape, F32),
            pltpu.SemaphoreType.DMA((2, len(cuts) - 1)),
            pltpu.SemaphoreType.DMA((2, len(cuts) - 1)),
        ],
        compiler_params=pltpu.CompilerParams(vmem_limit_bytes=VMEM),
        cost_estimate=pl.CostEstimate(flops=2 * (both * rows) ** 2 * each * count, bytes_accessed=10 * MIB, transcendentals=0),
        name="merge",
    )(force, in_hbm(res), in_hbm(tan))


def shards(displacement, direction, quad_nodes, quad_weights, gap_nominal, pressure_load, degrees):
    bands = lax.axis_size("space")
    count = 2 * lax.axis_size("mode")
    odd = (lax.axis_index("space") % 2).astype(jnp.int32).reshape(1)
    pairs = [[p * count + i for i in range(count)] for p in range(bands // 2)]

    def exchange(x):
        return lax.all_to_all(x, ("space", "mode"), split_axis=0, concat_axis=0, axis_index_groups=pairs, tiled=True)

    send = pack(displacement, direction, count)
    first, second, send = lax.optimization_barrier((displacement, direction, send))
    got = exchange(send)
    terms, ends = edges(odd, first, second, count)
    ends = lax.ppermute(ends, "space", [(i, i ^ 1) for i in range(bands)])
    res, tan = stencil(first), stencil(second)
    table = basis(quad_nodes, degrees)
    scale = quad_weights * pressure_load * (STEEP * STEEP)
    table_w = (table.astype(F32) * scale[None, :]).astype(BF16)
    turn = one_hot(jnp.equal(*iotas((table.shape[0],) * 2))) * (-STEEP)
    table_t = lax.dot_general(table, turn.astype(BF16), (((0,), (0,)), ((), ())), preferred_element_type=F32).astype(BF16)
    shift = jnp.broadcast_to((STEEP * (gap_nominal - FLOOR))[:, None], (gap_nominal.shape[0], 128))
    terms, res, tan, table_t, table_w, shift = lax.optimization_barrier((terms, res, tan, table_t, table_w, shift))
    outer = lax.ppermute(terms, "space", [(i + a, i + b) for i in range(1, bands - 1, 2) for a, b in ((0, 1), (1, 0))])
    got, ends = lax.optimization_barrier((got, ends))
    force = quad_forces(got, table_t, table_w, shift)
    back = exchange(force)
    res, tan = add_outer(odd, outer, ends, res, tan, count)
    return tuple(merge(back, res, tan))


def solution(mesh):
    in_specs = (P("mode", "space", None), P("mode", "space", None), P(), P(), P(), P(), P())
    out_specs = (P("mode", "space", None), P("mode", "space", None))
    return jax.shard_map(shards, mesh=mesh, in_specs=in_specs, out_specs=out_specs, check_vma=False)
```

```python
import functools

import jax
import jax.numpy as jnp
from jax import lax
from jax.experimental import pallas as pl
from jax.experimental.pallas import tpu as pltpu
from jax.sharding import PartitionSpec as P

HALF_ROOT = 0.7071067811865476
THIRD_NORM = 0.4082482904638631
FOURTH_NORM = 0.2041241452319315
FLOOR = 0.3
STEEP = 4.0
STIFF = 0.1
LOG2E = 1.4426950408889634
LN2 = 0.6931471805599453
MIB = 1 << 20
VMEM = 24 * MIB
F32 = jnp.float32
BF16 = jnp.bfloat16
HBM = pltpu.HBM


def basis(quad_nodes, degrees):
    points = quad_nodes[None, :, :]
    degree_grid = degrees[:, None, :]
    square = points * points
    third = (square * points - 3.0 * points) * THIRD_NORM
    fourth = (square * square - 6.0 * square + 3.0) * FOURTH_NORM
    second = (square - 1.0) * HALF_ROOT
    factor = jnp.where(
        degree_grid == 0,
        1.0,
        jnp.where(
            degree_grid == 1,
            points,
            jnp.where(degree_grid == 2, second, jnp.where(degree_grid == 3, third, fourth)),
        ),
    )
    return jnp.prod(factor, axis=2).astype(BF16)


def iotas(shape):
    return lax.broadcasted_iota(jnp.int32, shape, 0), lax.broadcasted_iota(jnp.int32, shape, 1)


def one_hot(hit):
    return jnp.where(hit, 1.0, 0.0).astype(BF16)


def in_hbm(x):
    return pltpu.with_memory_space_constraint(x, HBM)


def shifted(v, lane, by):
    width = v.shape[-1]
    inside = lane < width - 1 if by > 0 else lane > 0
    return jnp.where(inside, pltpu.roll(v, width - 1 if by > 0 else 1, 1), 0.0)


def pack_kernel(groups, early, step, disp_ref, dir_ref, send_ref, in_buf, out_buf, in_sem, out_sem):
    modes, rows, width = disp_ref.shape
    count, _, both, each = send_ref.shape
    size = both * rows
    per = count // groups
    span = per * each

    ahead = groups // early

    def loads(g):
        cols = pl.ds(g * ahead * span, ahead * span)
        return [
            pltpu.make_async_copy(ref.at[:, :, cols], in_buf.at[f, :, :, cols], in_sem.at[f, g])
            for f, ref in enumerate((disp_ref, dir_ref))
        ]

    def store(g):
        at = pl.ds(g * per, per)
        return pltpu.make_async_copy(out_buf.at[at], send_ref.at[at], out_sem.at[g])

    for g in range(early):
        for copy in loads(g):
            copy.start()
    to, frm = iotas((size, size))
    perm = one_hot(frm == (to % both) * rows + to // both)
    for g in range(groups):
        for copy in loads(g // ahead) if g % ahead == 0 else []:
            copy.wait()
        for d in range(g * per, (g + 1) * per, step):
            fields = in_buf[:, :, :, pl.ds(d * each, step * each)].reshape(size, step * each)
            moved = jnp.dot(perm, fields, preferred_element_type=F32).astype(BF16)
            for k in range(step):
                out_buf[d + k] = moved[:, k * each : (k + 1) * each].reshape(rows, both, each)
        store(g).start()
    for g in range(groups):
        store(g).wait()


def pack(displacement, direction, count, groups=4, early=2, step=2):
    modes, rows, width = displacement.shape
    each = width // count
    both = 2 * modes
    hbm = pl.BlockSpec(memory_space=HBM)
    shape = (count, rows, both, each)
    return pl.pallas_call(
        functools.partial(pack_kernel, groups, early, step),
        in_specs=[hbm, hbm],
        out_specs=hbm,
        out_shape=pltpu.HBM(shape, BF16),
        scratch_shapes=[
            pltpu.VMEM((2, modes, rows, width), BF16),
            pltpu.VMEM(shape, BF16),
            pltpu.SemaphoreType.DMA((2, early)),
            pltpu.SemaphoreType.DMA((groups,)),
        ],
        compiler_params=pltpu.CompilerParams(vmem_limit_bytes=VMEM),
        cost_estimate=pl.CostEstimate(flops=2 * (2 * modes * rows) ** 2 * width, bytes_accessed=4 * MIB, transcendentals=0),
        name="pack",
    )(in_hbm(displacement), in_hbm(direction))


def quad_kernel(chunk, deep, got_ref, table_t_ref, table_w_ref, shift_ref, out_ref, out_buf, w_ref, cross_ref, out_sem):
    count, rows, both, each = got_ref.shape
    per = count // 2
    modes = both // 2
    quad = table_t_ref.shape[0]
    total = per * modes
    pairs = rows // deep
    steps = 2 * pairs

    def store(i):
        at = pl.ds(i // pairs * per, per)
        lines = pl.ds(i % pairs * deep, deep)
        return pltpu.make_async_copy(out_buf.at[at, lines], out_ref.at[at, lines], out_sem.at[i])

    def field_rows(i, f):
        at = pl.ds(i // pairs * per, per)
        lines = [
            got_ref[at, i % pairs * deep + k, f * modes : (f + 1) * modes, :].reshape(total, each) for k in range(deep)
        ]
        return jnp.concatenate(lines, axis=1)

    frm, to = iotas((deep * each, deep * each))
    far = frm % each - to % each
    for band in range(2):
        near = frm // each == band
        full = to // each == 1 - band
        value = jnp.where(far == 0, jnp.where(near, jnp.where(full, -8.0, 1.0), jnp.where(full, 1.0, 0.0)), 0.0)
        cross_ref[band] = jnp.where((jnp.abs(far) == 1) & near & full, 2.0, value).astype(BF16)

    def forward(i, slots):
        slot = i % 2
        disp = field_rows(i, 0)
        dire = field_rows(i, 1)
        for q in range(quad // chunk):
            at = pl.ds(q * chunk, chunk)
            left = table_t_ref[at, :]
            shift = shift_ref[at, :]
            shift = jnp.concatenate([shift] * (deep * each // shift.shape[1]), axis=1)
            s = shift + jnp.dot(left, disp, preferred_element_type=F32)
            probe = jnp.dot(left, dire, preferred_element_type=F32)
            e = jnp.exp2(jnp.minimum(s, 80.0) * LOG2E)
            one = 1.0 + e
            big = jnp.maximum(s, jnp.log2(one) * LN2) + STEEP * FLOOR
            inv = pl.reciprocal(big, approx=True)
            sig = e * pl.reciprocal(one, approx=True)
            square = inv * inv
            w_ref[slot, 0, at, :] = square.astype(BF16)
            w_ref[slot, 1, at, :] = ((sig * inv) * (square * probe)).astype(BF16)
            if i > 0 and q in slots:
                back(i - 1, slots[q])

    def back(i, f):
        band, pair = i // pairs, i % pairs
        factor = (-STIFF, 0.5 * STIFF)[f]
        force = jnp.dot(table_w_ref[...], w_ref[i % 2, f], preferred_element_type=F32)
        if i in (pairs - 1, pairs):
            facing = field_rows(steps - 1 - i, f)
            force = force + factor * jnp.dot(facing, cross_ref[band], preferred_element_type=F32)
        force = force.astype(BF16)
        for k in range(deep):
            part = force[:, k * each : (k + 1) * each].reshape(per, modes, each)
            out_buf[band * per : (band + 1) * per, pair * deep + k, f * modes : (f + 1) * modes, :] = part

    slots = {quad // chunk // 2 - 1: 0, quad // chunk - 1: 1}
    for i in range(steps):
        forward(i, slots)
        if i > 0:
            store(i - 1).start()
    for f in range(2):
        back(steps - 1, f)
    store(steps - 1).start()
    for i in range(steps):
        store(i).wait()


def quad_forces(got, table_t, table_w, shift, deep=2):
    count, rows, both, each = got.shape
    quad, total = table_t.shape
    vmem = pl.BlockSpec(memory_space=pltpu.VMEM)
    return pl.pallas_call(
        functools.partial(quad_kernel, 128, deep),
        in_specs=[vmem] * 4,
        out_specs=pl.BlockSpec(memory_space=HBM),
        out_shape=pltpu.HBM(got.shape, BF16),
        scratch_shapes=[
            pltpu.VMEM(got.shape, BF16),
            pltpu.VMEM((2, 2, quad, deep * each), BF16),
            pltpu.VMEM((2, deep * each, deep * each), BF16),
            pltpu.SemaphoreType.DMA((2 * rows // deep,)),
        ],
        compiler_params=pltpu.CompilerParams(vmem_limit_bytes=VMEM),
        cost_estimate=pl.CostEstimate(flops=3 << 31, bytes_accessed=1 << 10, transcendentals=0),
        name="quad_forces",
    )(got, table_t, table_w, shift)


def stencil_kernel(chunk, x_ref, out_ref, inner_ref, side_ref):
    modes, rows, width = x_ref.shape
    size = modes * rows
    to, frm = iotas((size, size))
    gap = jnp.abs(to - frm)
    same = to // rows == frm // rows
    centre = jnp.where(gap == 0, 20.0, jnp.where(gap == 1, -8.0, jnp.where(gap == 2, 1.0, 0.0)))
    centre = jnp.where(same, centre, 0.0).astype(BF16)
    side = jnp.where(gap == 0, -8.0, jnp.where(gap == 1, 2.0, 0.0))
    side = jnp.where(same, side, 0.0).astype(BF16)
    for c in range(width // chunk):
        cols = pl.ds(c * chunk, chunk)
        x = x_ref[:, :, cols].reshape(size, chunk)
        inner_ref[:, :, cols] = jnp.dot(centre, x, preferred_element_type=F32).reshape(modes, rows, chunk)
        side_ref[:, :, cols] = jnp.dot(side, x, preferred_element_type=F32).reshape(modes, rows, chunk)
    lane = lax.broadcasted_iota(jnp.int32, (rows, width), 1)

    def one_mode(m, _):
        x = x_ref[m].astype(F32)
        y = side_ref[m]
        right = shifted(y + shifted(x, lane, 1), lane, 1)
        left = shifted(y + shifted(x, lane, -1), lane, -1)
        out_ref[m] = (STIFF * (inner_ref[m] + right + left)).astype(BF16)
        return 0

    lax.fori_loop(0, modes, one_mode, 0)


def stencil(x):
    whole = pl.BlockSpec(x.shape, lambda i: (0, 0, 0))
    return pl.pallas_call(
        functools.partial(stencil_kernel, 512),
        grid=(1,),
        in_specs=[whole],
        out_specs=whole,
        out_shape=pltpu.HBM(x.shape, BF16),
        scratch_shapes=[pltpu.VMEM(x.shape, F32)] * 2,
        compiler_params=pltpu.CompilerParams(vmem_limit_bytes=VMEM),
        cost_estimate=pl.CostEstimate(flops=1 << 30, bytes_accessed=1 << 20, transcendentals=0),
        name="stencil",
    )(in_hbm(x))


def outer_kernel(block, blocks, odd_ref, outer_ref, ends_ref, res_ref, tan_ref, res_out, tan_out):
    modes, rows, chunk = res_ref.shape
    size = modes * rows
    odd = odd_ref[0]
    to, frm = iotas((size, modes))
    corner = one_hot((frm == to // rows) & (to % rows == (rows - 1) * (1 - odd)))
    item, col = iotas((ends_ref.shape[1], chunk))
    target = jnp.where(item < blocks, item * block - 1, (item - blocks + 1) * block)
    target = jnp.where(item < 2 * blocks, target, -1)
    spread = jnp.dot(ends_ref[...], one_hot(target == col + pl.program_id(0) * chunk), preferred_element_type=F32).astype(BF16)
    to, frm = iotas((size, 2 * modes))
    place = one_hot((frm % modes == to // rows) & (to % rows == frm // modes + (rows - 2) * odd))
    for f, (ref, out) in enumerate(((res_ref, res_out), (tan_ref, tan_out))):
        terms = outer_ref[:, f * modes : (f + 1) * modes, :].reshape(2 * modes, chunk)
        terms = jnp.dot(place, terms, preferred_element_type=F32)
        corners = jnp.dot(corner, spread[f * modes : (f + 1) * modes], preferred_element_type=F32)
        terms = (terms + (2.0 * STIFF) * corners).reshape(modes, rows, chunk)
        out[...] = (ref[...].astype(F32) + terms).astype(BF16)


def add_outer(odd, outer, ends, res, tan, count, steps=4):
    modes, rows, width = res.shape
    field = pl.BlockSpec((modes, rows, width // steps), lambda i: (0, 0, i))
    return pl.pallas_call(
        functools.partial(outer_kernel, width // count, count),
        grid=(steps,),
        in_specs=[
            pl.BlockSpec(memory_space=pltpu.SMEM),
            pl.BlockSpec((2, 2 * modes, width // steps), lambda i: (0, 0, i)),
            pl.BlockSpec(ends.shape, lambda i: (0, 0)),
            field,
            field,
        ],
        out_specs=[field, field],
        out_shape=[pltpu.HBM(res.shape, BF16)] * 2,
        compiler_params=pltpu.CompilerParams(vmem_limit_bytes=VMEM),
        cost_estimate=pl.CostEstimate(flops=5 << 32, bytes_accessed=7 * MIB, transcendentals=0),
        name="add_outer",
    )(odd, outer, ends, in_hbm(res), in_hbm(tan))


def edges_kernel(block, odd_ref, disp_ref, dir_ref, terms_ref, ends_ref):
    modes, rows, width = disp_ref.shape
    size = modes * rows
    blocks = width // block
    odd = odd_ref[0]
    outer = (rows - 1) * odd
    inner = jnp.where(odd == 1, rows - 2, 1)
    to, frm = iotas((2 * modes, size))
    same = to % modes == frm // rows
    row = frm % rows
    full = to // modes == 1 - odd
    plain = jnp.where(row == outer, jnp.where(full, -8.0, 1.0), jnp.where(full & (row == inner), 1.0, 0.0))
    plain = jnp.where(same, plain, 0.0).astype(BF16)
    to, frm = iotas((modes, size))
    same = to == frm // rows
    corner = jnp.where(same & (frm % rows == outer), 2.0, 0.0).astype(BF16)
    facing = one_hot(same & (frm % rows == rows - 1 - outer))
    lane = lax.broadcasted_iota(jnp.int32, (modes, width), 1)
    col, item = iotas((width, ends_ref.shape[1]))
    source = jnp.where(item < blocks, item * block, (item - blocks) * block + block - 1)
    pick = one_hot((col == source) & (item < 2 * blocks))
    first = jnp.where(odd == 1, 1.0, 0.0)
    for f, ref in enumerate((disp_ref, dir_ref)):
        at = pl.ds(f * modes, modes)
        x = ref[...].reshape(size, width)
        terms = jnp.dot(plain, x, preferred_element_type=F32)
        corners = jnp.dot(corner, x, preferred_element_type=F32)
        corners = shifted(corners, lane, 1) + shifted(corners, lane, -1)
        terms_ref[0, at, :] = (STIFF * (terms[:modes] + first * corners)).astype(BF16)
        terms_ref[1, at, :] = (STIFF * (terms[modes:] + (1.0 - first) * corners)).astype(BF16)
        line = jnp.dot(facing, x, preferred_element_type=F32).astype(BF16)
        ends_ref[at, :] = jnp.dot(line, pick, preferred_element_type=F32).astype(BF16)


def edges(odd, displacement, direction, count):
    modes, rows, width = displacement.shape
    lanes = max(128, 2 * count)
    whole = pl.BlockSpec(displacement.shape, lambda i: (0, 0, 0))
    return pl.pallas_call(
        functools.partial(edges_kernel, width // count),
        grid=(1,),
        in_specs=[pl.BlockSpec(memory_space=pltpu.SMEM), whole, whole],
        out_specs=[
            pl.BlockSpec((2, 2 * modes, width), lambda i: (0, 0, 0)),
            pl.BlockSpec((2 * modes, lanes), lambda i: (0, 0)),
        ],
        out_shape=[pltpu.HBM((2, 2 * modes, width), BF16), pltpu.HBM((2 * modes, lanes), BF16)],
        compiler_params=pltpu.CompilerParams(vmem_limit_bytes=VMEM),
        cost_estimate=pl.CostEstimate(flops=1 << 20, bytes_accessed=1 << 20, transcendentals=0),
        name="edges",
    )(odd, in_hbm(displacement), in_hbm(direction))


def merge_kernel(cuts, step, force_ref, res_ref, tan_ref, res_out, tan_out, in_buf, buf, in_sem, out_sem):
    count, rows, both, each = force_ref.shape
    modes = both // 2
    size = both * rows
    groups = len(cuts) - 1
    span = step * each

    def loads(g):
        cols = pl.ds(cuts[g] * span, (cuts[g + 1] - cuts[g]) * span)
        return [
            pltpu.make_async_copy(ref.at[:, :, cols], in_buf.at[f, :, :, cols], in_sem.at[f, g])
            for f, ref in enumerate((res_ref, tan_ref))
        ]

    def stores(g):
        cols = pl.ds(cuts[g] * span, (cuts[g + 1] - cuts[g]) * span)
        return [
            pltpu.make_async_copy(buf.at[f, :, :, cols], ref.at[:, :, cols], out_sem.at[f, g])
            for f, ref in enumerate((res_out, tan_out))
        ]

    for g in range(groups):
        for copy in loads(g):
            copy.start()
    to, frm = iotas((size, size))
    hit = (to % rows == frm // both) & (to // rows == frm % both)
    moves = jnp.where(hit, jnp.where(to // rows < modes, -1.0, 2.0), 0.0).astype(BF16)
    def moved(t):
        force = [force_ref[t * step + k].reshape(size, each) for k in range(step)]
        terms = jnp.dot(moves, jnp.concatenate(force, axis=1), preferred_element_type=F32)
        return terms.reshape(2, modes, rows, span)

    for t in range(cuts[1]):
        buf[:, :, :, pl.ds(t * span, span)] = moved(t)
    for g in range(groups):
        for copy in loads(g):
            copy.wait()
        for t in range(cuts[g], cuts[g + 1]):
            cols = pl.ds(t * span, span)
            terms = buf[:, :, :, cols] if g == 0 else moved(t)
            buf[:, :, :, cols] = in_buf[:, :, :, cols].astype(F32) + terms
        for copy in stores(g):
            copy.start()
    for g in range(groups):
        for copy in stores(g):
            copy.wait()


def merge(force, res, tan, cuts=(0, 4, 8, 12, 16), step=2):
    count, rows, both, each = force.shape
    vmem = pl.BlockSpec(memory_space=pltpu.VMEM)
    hbm = pl.BlockSpec(memory_space=HBM)
    return pl.pallas_call(
        functools.partial(merge_kernel, cuts, step),
        in_specs=[vmem, hbm, hbm],
        out_specs=[hbm] * 2,
        out_shape=[pltpu.HBM(res.shape, F32)] * 2,
        scratch_shapes=[
            pltpu.VMEM((2,) + res.shape, BF16),
            pltpu.VMEM((2,) + res.shape, F32),
            pltpu.SemaphoreType.DMA((2, len(cuts) - 1)),
            pltpu.SemaphoreType.DMA((2, len(cuts) - 1)),
        ],
        compiler_params=pltpu.CompilerParams(vmem_limit_bytes=VMEM),
        cost_estimate=pl.CostEstimate(flops=2 * (both * rows) ** 2 * each * count, bytes_accessed=10 * MIB, transcendentals=0),
        name="merge",
    )(force, in_hbm(res), in_hbm(tan))


def shards(displacement, direction, quad_nodes, quad_weights, gap_nominal, pressure_load, degrees):
    bands = lax.axis_size("space")
    count = 2 * lax.axis_size("mode")
    odd = (lax.axis_index("space") % 2).astype(jnp.int32).reshape(1)
    pairs = [[p * count + i for i in range(count)] for p in range(bands // 2)]

    def exchange(x):
        return lax.all_to_all(x, ("space", "mode"), split_axis=0, concat_axis=0, axis_index_groups=pairs, tiled=True)

    send = pack(displacement, direction, count)
    first, second, send = lax.optimization_barrier((displacement, direction, send))
    got = exchange(send)
    terms, ends = edges(odd, first, second, count)
    ends = lax.ppermute(ends, "space", [(i, i ^ 1) for i in range(bands)])
    res, tan = stencil(first), stencil(second)
    table = basis(quad_nodes, degrees)
    scale = quad_weights * pressure_load * (STEEP * STEEP)
    table_w = (table.astype(F32) * scale[None, :]).astype(BF16)
    turn = one_hot(jnp.equal(*iotas((table.shape[0],) * 2))) * (-STEEP)
    table_t = lax.dot_general(table, turn.astype(BF16), (((0,), (0,)), ((), ())), preferred_element_type=F32).astype(BF16)
    shift = jnp.broadcast_to((STEEP * (gap_nominal - FLOOR))[:, None], (gap_nominal.shape[0], 128))
    terms, res, tan, table_t, table_w, shift = lax.optimization_barrier((terms, res, tan, table_t, table_w, shift))
    outer = lax.ppermute(terms, "space", [(i + a, i + b) for i in range(1, bands - 1, 2) for a, b in ((0, 1), (1, 0))])
    got, ends = lax.optimization_barrier((got, ends))
    force = quad_forces(got, table_t, table_w, shift)
    back = exchange(force)
    res, tan = add_outer(odd, outer, ends, res, tan, count)
    return tuple(merge(back, res, tan))


def solution(mesh):
    in_specs = (P("mode", "space", None), P("mode", "space", None), P(), P(), P(), P(), P())
    out_specs = (P("mode", "space", None), P("mode", "space", None))
    return jax.shard_map(shards, mesh=mesh, in_specs=in_specs, out_specs=out_specs, check_vma=False)
```

```python
import functools

import jax
import jax.numpy as jnp
from jax import lax
from jax.experimental import pallas as pl
from jax.experimental.pallas import tpu as pltpu
from jax.sharding import PartitionSpec as P

HALF_ROOT = 0.7071067811865476
THIRD_NORM = 0.4082482904638631
FOURTH_NORM = 0.2041241452319315
FLOOR = 0.3
STEEP = 4.0
STIFF = 0.1
LOG2E = 1.4426950408889634
LN2 = 0.6931471805599453
MIB = 1 << 20
VMEM = 24 * MIB
F32 = jnp.float32
BF16 = jnp.bfloat16
HBM = pltpu.HBM


def basis(quad_nodes, degrees):
    points = quad_nodes[None, :, :]
    degree_grid = degrees[:, None, :]
    square = points * points
    third = (square * points - 3.0 * points) * THIRD_NORM
    fourth = (square * square - 6.0 * square + 3.0) * FOURTH_NORM
    second = (square - 1.0) * HALF_ROOT
    factor = jnp.where(
        degree_grid == 0,
        1.0,
        jnp.where(
            degree_grid == 1,
            points,
            jnp.where(degree_grid == 2, second, jnp.where(degree_grid == 3, third, fourth)),
        ),
    )
    return jnp.prod(factor, axis=2).astype(BF16)


def iotas(shape):
    return lax.broadcasted_iota(jnp.int32, shape, 0), lax.broadcasted_iota(jnp.int32, shape, 1)


def one_hot(hit):
    return jnp.where(hit, 1.0, 0.0).astype(BF16)


def in_hbm(x):
    return pltpu.with_memory_space_constraint(x, HBM)


def shifted(v, lane, by):
    width = v.shape[-1]
    inside = lane < width - 1 if by > 0 else lane > 0
    return jnp.where(inside, pltpu.roll(v, width - 1 if by > 0 else 1, 1), 0.0)


def pack_kernel(groups, early, step, disp_ref, dir_ref, send_ref, in_buf, out_buf, in_sem, out_sem):
    modes, rows, width = disp_ref.shape
    count, _, both, each = send_ref.shape
    size = both * rows
    per = count // groups
    span = per * each

    ahead = groups // early

    def loads(g):
        cols = pl.ds(g * ahead * span, ahead * span)
        return [
            pltpu.make_async_copy(ref.at[:, :, cols], in_buf.at[f, :, :, cols], in_sem.at[f, g])
            for f, ref in enumerate((disp_ref, dir_ref))
        ]

    def store(g):
        at = pl.ds(g * per, per)
        return pltpu.make_async_copy(out_buf.at[at], send_ref.at[at], out_sem.at[g])

    for g in range(early):
        for copy in loads(g):
            copy.start()
    to, frm = iotas((size, size))
    perm = one_hot(frm == (to % both) * rows + to // both)
    for g in range(groups):
        for copy in loads(g // ahead) if g % ahead == 0 else []:
            copy.wait()
        for d in range(g * per, (g + 1) * per, step):
            fields = in_buf[:, :, :, pl.ds(d * each, step * each)].reshape(size, step * each)
            moved = jnp.dot(perm, fields, preferred_element_type=F32).astype(BF16)
            for k in range(step):
                out_buf[d + k] = moved[:, k * each : (k + 1) * each].reshape(rows, both, each)
        store(g).start()
    for g in range(groups):
        store(g).wait()


def pack(displacement, direction, count, groups=4, early=2, step=2):
    modes, rows, width = displacement.shape
    each = width // count
    both = 2 * modes
    hbm = pl.BlockSpec(memory_space=HBM)
    shape = (count, rows, both, each)
    return pl.pallas_call(
        functools.partial(pack_kernel, groups, early, step),
        in_specs=[hbm, hbm],
        out_specs=hbm,
        out_shape=pltpu.HBM(shape, BF16),
        scratch_shapes=[
            pltpu.VMEM((2, modes, rows, width), BF16),
            pltpu.VMEM(shape, BF16),
            pltpu.SemaphoreType.DMA((2, early)),
            pltpu.SemaphoreType.DMA((groups,)),
        ],
        compiler_params=pltpu.CompilerParams(vmem_limit_bytes=VMEM),
        cost_estimate=pl.CostEstimate(flops=2 * (2 * modes * rows) ** 2 * width, bytes_accessed=4 * MIB, transcendentals=0),
        name="pack",
    )(in_hbm(displacement), in_hbm(direction))


def quad_kernel(chunk, deep, got_ref, table_t_ref, table_w_ref, shift_ref, out_ref, out_buf, w_ref, cross_ref, out_sem):
    count, rows, both, each = got_ref.shape
    per = count // 2
    modes = both // 2
    quad = table_t_ref.shape[0]
    total = per * modes
    pairs = rows // deep
    steps = 2 * pairs

    def store(i):
        at = pl.ds(i // pairs * per, per)
        lines = pl.ds(i % pairs * deep, deep)
        return pltpu.make_async_copy(out_buf.at[at, lines], out_ref.at[at, lines], out_sem.at[i])

    def last_half(f):
        here = (pl.ds(per, per), pl.ds(rows - deep, deep), pl.ds(f * modes, modes))
        return pltpu.make_async_copy(out_buf.at[here], out_ref.at[here], out_sem.at[steps - 1 + f])

    def field_rows(i, f):
        at = pl.ds(i // pairs * per, per)
        lines = [
            got_ref[at, i % pairs * deep + k, f * modes : (f + 1) * modes, :].reshape(total, each) for k in range(deep)
        ]
        return jnp.concatenate(lines, axis=1)

    frm, to = iotas((deep * each, deep * each))
    far = frm % each - to % each
    for band in range(2):
        near = frm // each == band
        full = to // each == 1 - band
        value = jnp.where(far == 0, jnp.where(near, jnp.where(full, -8.0, 1.0), jnp.where(full, 1.0, 0.0)), 0.0)
        cross_ref[band] = jnp.where((jnp.abs(far) == 1) & near & full, 2.0, value).astype(BF16)

    def forward(i, slots):
        slot = i % 2
        disp = field_rows(i, 0)
        dire = field_rows(i, 1)
        for q in range(quad // chunk):
            at = pl.ds(q * chunk, chunk)
            left = table_t_ref[at, :]
            shift = shift_ref[at, :]
            shift = jnp.concatenate([shift] * (deep * each // shift.shape[1]), axis=1)
            s = shift + jnp.dot(left, disp, preferred_element_type=F32)
            probe = jnp.dot(left, dire, preferred_element_type=F32)
            e = jnp.exp2(jnp.minimum(s, 80.0) * LOG2E)
            one = 1.0 + e
            big = jnp.maximum(s, jnp.log2(one) * LN2) + STEEP * FLOOR
            inv = pl.reciprocal(big, approx=True)
            sig = e * pl.reciprocal(one, approx=True)
            square = inv * inv
            w_ref[slot, 0, at, :] = square.astype(BF16)
            w_ref[slot, 1, at, :] = ((sig * inv) * (square * probe)).astype(BF16)
            if i > 0 and q in slots:
                back(i - 1, slots[q])

    def back(i, f):
        band, pair = i // pairs, i % pairs
        factor = (-STIFF, 0.5 * STIFF)[f]
        force = jnp.dot(table_w_ref[...], w_ref[i % 2, f], preferred_element_type=F32)
        if i in (pairs - 1, pairs):
            facing = field_rows(steps - 1 - i, f)
            force = force + factor * jnp.dot(facing, cross_ref[band], preferred_element_type=F32)
        force = force.astype(BF16)
        for k in range(deep):
            part = force[:, k * each : (k + 1) * each].reshape(per, modes, each)
            out_buf[band * per : (band + 1) * per, pair * deep + k, f * modes : (f + 1) * modes, :] = part

    slots = {quad // chunk // 2 - 1: 0, quad // chunk - 1: 1}
    for i in range(steps):
        forward(i, slots)
        if i > 0:
            store(i - 1).start()
    for f in range(2):
        back(steps - 1, f)
        last_half(f).start()
    for i in range(steps - 1):
        store(i).wait()
    for f in range(2):
        last_half(f).wait()


def quad_forces(got, table_t, table_w, shift, deep=2):
    count, rows, both, each = got.shape
    quad, total = table_t.shape
    vmem = pl.BlockSpec(memory_space=pltpu.VMEM)
    return pl.pallas_call(
        functools.partial(quad_kernel, 128, deep),
        in_specs=[vmem] * 4,
        out_specs=pl.BlockSpec(memory_space=HBM),
        out_shape=pltpu.HBM(got.shape, BF16),
        scratch_shapes=[
            pltpu.VMEM(got.shape, BF16),
            pltpu.VMEM((2, 2, quad, deep * each), BF16),
            pltpu.VMEM((2, deep * each, deep * each), BF16),
            pltpu.SemaphoreType.DMA((2 * rows // deep + 1,)),
        ],
        compiler_params=pltpu.CompilerParams(vmem_limit_bytes=VMEM),
        cost_estimate=pl.CostEstimate(flops=3 << 31, bytes_accessed=1 << 10, transcendentals=0),
        name="quad_forces",
    )(got, table_t, table_w, shift)


def stencil_kernel(chunk, x_ref, out_ref, inner_ref, side_ref):
    modes, rows, width = x_ref.shape
    size = modes * rows
    to, frm = iotas((size, size))
    gap = jnp.abs(to - frm)
    same = to // rows == frm // rows
    centre = jnp.where(gap == 0, 20.0, jnp.where(gap == 1, -8.0, jnp.where(gap == 2, 1.0, 0.0)))
    centre = jnp.where(same, centre, 0.0).astype(BF16)
    side = jnp.where(gap == 0, -8.0, jnp.where(gap == 1, 2.0, 0.0))
    side = jnp.where(same, side, 0.0).astype(BF16)
    for c in range(width // chunk):
        cols = pl.ds(c * chunk, chunk)
        x = x_ref[:, :, cols].reshape(size, chunk)
        inner_ref[:, :, cols] = jnp.dot(centre, x, preferred_element_type=F32).reshape(modes, rows, chunk)
        side_ref[:, :, cols] = jnp.dot(side, x, preferred_element_type=F32).reshape(modes, rows, chunk)
    lane = lax.broadcasted_iota(jnp.int32, (rows, width), 1)

    def one_mode(m, _):
        x = x_ref[m].astype(F32)
        y = side_ref[m]
        right = shifted(y + shifted(x, lane, 1), lane, 1)
        left = shifted(y + shifted(x, lane, -1), lane, -1)
        out_ref[m] = (STIFF * (inner_ref[m] + right + left)).astype(BF16)
        return 0

    lax.fori_loop(0, modes, one_mode, 0)


def stencil(x):
    whole = pl.BlockSpec(x.shape, lambda i: (0, 0, 0))
    return pl.pallas_call(
        functools.partial(stencil_kernel, 512),
        grid=(1,),
        in_specs=[whole],
        out_specs=whole,
        out_shape=pltpu.HBM(x.shape, BF16),
        scratch_shapes=[pltpu.VMEM(x.shape, F32)] * 2,
        compiler_params=pltpu.CompilerParams(vmem_limit_bytes=VMEM),
        cost_estimate=pl.CostEstimate(flops=1 << 30, bytes_accessed=1 << 20, transcendentals=0),
        name="stencil",
    )(in_hbm(x))


def outer_kernel(block, blocks, odd_ref, outer_ref, ends_ref, res_ref, tan_ref, res_out, tan_out):
    modes, rows, chunk = res_ref.shape
    size = modes * rows
    odd = odd_ref[0]
    to, frm = iotas((size, modes))
    corner = one_hot((frm == to // rows) & (to % rows == (rows - 1) * (1 - odd)))
    item, col = iotas((ends_ref.shape[1], chunk))
    target = jnp.where(item < blocks, item * block - 1, (item - blocks + 1) * block)
    target = jnp.where(item < 2 * blocks, target, -1)
    spread = jnp.dot(ends_ref[...], one_hot(target == col + pl.program_id(0) * chunk), preferred_element_type=F32).astype(BF16)
    to, frm = iotas((size, 2 * modes))
    place = one_hot((frm % modes == to // rows) & (to % rows == frm // modes + (rows - 2) * odd))
    for f, (ref, out) in enumerate(((res_ref, res_out), (tan_ref, tan_out))):
        terms = outer_ref[:, f * modes : (f + 1) * modes, :].reshape(2 * modes, chunk)
        terms = jnp.dot(place, terms, preferred_element_type=F32)
        corners = jnp.dot(corner, spread[f * modes : (f + 1) * modes], preferred_element_type=F32)
        terms = (terms + (2.0 * STIFF) * corners).reshape(modes, rows, chunk)
        out[...] = (ref[...].astype(F32) + terms).astype(BF16)


def add_outer(odd, outer, ends, res, tan, count, steps=4):
    modes, rows, width = res.shape
    field = pl.BlockSpec((modes, rows, width // steps), lambda i: (0, 0, i))
    return pl.pallas_call(
        functools.partial(outer_kernel, width // count, count),
        grid=(steps,),
        in_specs=[
            pl.BlockSpec(memory_space=pltpu.SMEM),
            pl.BlockSpec((2, 2 * modes, width // steps), lambda i: (0, 0, i)),
            pl.BlockSpec(ends.shape, lambda i: (0, 0)),
            field,
            field,
        ],
        out_specs=[field, field],
        out_shape=[pltpu.HBM(res.shape, BF16)] * 2,
        compiler_params=pltpu.CompilerParams(vmem_limit_bytes=VMEM),
        cost_estimate=pl.CostEstimate(flops=5 << 32, bytes_accessed=7 * MIB, transcendentals=0),
        name="add_outer",
    )(odd, outer, ends, in_hbm(res), in_hbm(tan))


def edges_kernel(block, odd_ref, disp_ref, dir_ref, terms_ref, ends_ref):
    modes, rows, width = disp_ref.shape
    size = modes * rows
    blocks = width // block
    odd = odd_ref[0]
    outer = (rows - 1) * odd
    inner = jnp.where(odd == 1, rows - 2, 1)
    to, frm = iotas((2 * modes, size))
    same = to % modes == frm // rows
    row = frm % rows
    full = to // modes == 1 - odd
    plain = jnp.where(row == outer, jnp.where(full, -8.0, 1.0), jnp.where(full & (row == inner), 1.0, 0.0))
    plain = jnp.where(same, plain, 0.0).astype(BF16)
    to, frm = iotas((modes, size))
    same = to == frm // rows
    corner = jnp.where(same & (frm % rows == outer), 2.0, 0.0).astype(BF16)
    facing = one_hot(same & (frm % rows == rows - 1 - outer))
    lane = lax.broadcasted_iota(jnp.int32, (modes, width), 1)
    col, item = iotas((width, ends_ref.shape[1]))
    source = jnp.where(item < blocks, item * block, (item - blocks) * block + block - 1)
    pick = one_hot((col == source) & (item < 2 * blocks))
    first = jnp.where(odd == 1, 1.0, 0.0)
    for f, ref in enumerate((disp_ref, dir_ref)):
        at = pl.ds(f * modes, modes)
        x = ref[...].reshape(size, width)
        terms = jnp.dot(plain, x, preferred_element_type=F32)
        corners = jnp.dot(corner, x, preferred_element_type=F32)
        corners = shifted(corners, lane, 1) + shifted(corners, lane, -1)
        terms_ref[0, at, :] = (STIFF * (terms[:modes] + first * corners)).astype(BF16)
        terms_ref[1, at, :] = (STIFF * (terms[modes:] + (1.0 - first) * corners)).astype(BF16)
        line = jnp.dot(facing, x, preferred_element_type=F32).astype(BF16)
        ends_ref[at, :] = jnp.dot(line, pick, preferred_element_type=F32).astype(BF16)


def edges(odd, displacement, direction, count):
    modes, rows, width = displacement.shape
    lanes = max(128, 2 * count)
    whole = pl.BlockSpec(displacement.shape, lambda i: (0, 0, 0))
    return pl.pallas_call(
        functools.partial(edges_kernel, width // count),
        grid=(1,),
        in_specs=[pl.BlockSpec(memory_space=pltpu.SMEM), whole, whole],
        out_specs=[
            pl.BlockSpec((2, 2 * modes, width), lambda i: (0, 0, 0)),
            pl.BlockSpec((2 * modes, lanes), lambda i: (0, 0)),
        ],
        out_shape=[pltpu.HBM((2, 2 * modes, width), BF16), pltpu.HBM((2 * modes, lanes), BF16)],
        compiler_params=pltpu.CompilerParams(vmem_limit_bytes=VMEM),
        cost_estimate=pl.CostEstimate(flops=1 << 20, bytes_accessed=1 << 20, transcendentals=0),
        name="edges",
    )(odd, in_hbm(displacement), in_hbm(direction))


def merge_kernel(cuts, step, force_ref, res_ref, tan_ref, res_out, tan_out, in_buf, buf, in_sem, out_sem):
    count, rows, both, each = force_ref.shape
    modes = both // 2
    size = both * rows
    groups = len(cuts) - 1
    span = step * each

    def loads(g):
        cols = pl.ds(cuts[g] * span, (cuts[g + 1] - cuts[g]) * span)
        return [
            pltpu.make_async_copy(ref.at[:, :, cols], in_buf.at[f, :, :, cols], in_sem.at[f, g])
            for f, ref in enumerate((res_ref, tan_ref))
        ]

    def stores(g):
        cols = pl.ds(cuts[g] * span, (cuts[g + 1] - cuts[g]) * span)
        return [
            pltpu.make_async_copy(buf.at[f, :, :, cols], ref.at[:, :, cols], out_sem.at[f, g])
            for f, ref in enumerate((res_out, tan_out))
        ]

    for g in range(groups):
        for copy in loads(g):
            copy.start()
    to, frm = iotas((size, size))
    hit = (to % rows == frm // both) & (to // rows == frm % both)
    moves = jnp.where(hit, jnp.where(to // rows < modes, -1.0, 2.0), 0.0).astype(BF16)
    def moved(t):
        force = [force_ref[t * step + k].reshape(size, each) for k in range(step)]
        terms = jnp.dot(moves, jnp.concatenate(force, axis=1), preferred_element_type=F32)
        return terms.reshape(2, modes, rows, span)

    for t in range(cuts[1]):
        buf[:, :, :, pl.ds(t * span, span)] = moved(t)
    for g in range(groups):
        for copy in loads(g):
            copy.wait()
        for t in range(cuts[g], cuts[g + 1]):
            cols = pl.ds(t * span, span)
            terms = buf[:, :, :, cols] if g == 0 else moved(t)
            buf[:, :, :, cols] = in_buf[:, :, :, cols].astype(F32) + terms
        for copy in stores(g):
            copy.start()
    for g in range(groups):
        for copy in stores(g):
            copy.wait()


def merge(force, res, tan, cuts=(0, 4, 8, 12, 16), step=2):
    count, rows, both, each = force.shape
    vmem = pl.BlockSpec(memory_space=pltpu.VMEM)
    hbm = pl.BlockSpec(memory_space=HBM)
    return pl.pallas_call(
        functools.partial(merge_kernel, cuts, step),
        in_specs=[vmem, hbm, hbm],
        out_specs=[hbm] * 2,
        out_shape=[pltpu.HBM(res.shape, F32)] * 2,
        scratch_shapes=[
            pltpu.VMEM((2,) + res.shape, BF16),
            pltpu.VMEM((2,) + res.shape, F32),
            pltpu.SemaphoreType.DMA((2, len(cuts) - 1)),
            pltpu.SemaphoreType.DMA((2, len(cuts) - 1)),
        ],
        compiler_params=pltpu.CompilerParams(vmem_limit_bytes=VMEM),
        cost_estimate=pl.CostEstimate(flops=2 * (both * rows) ** 2 * each * count, bytes_accessed=10 * MIB, transcendentals=0),
        name="merge",
    )(force, in_hbm(res), in_hbm(tan))


def shards(displacement, direction, quad_nodes, quad_weights, gap_nominal, pressure_load, degrees):
    bands = lax.axis_size("space")
    count = 2 * lax.axis_size("mode")
    odd = (lax.axis_index("space") % 2).astype(jnp.int32).reshape(1)
    pairs = [[p * count + i for i in range(count)] for p in range(bands // 2)]

    def exchange(x):
        return lax.all_to_all(x, ("space", "mode"), split_axis=0, concat_axis=0, axis_index_groups=pairs, tiled=True)

    send = pack(displacement, direction, count)
    first, second, send = lax.optimization_barrier((displacement, direction, send))
    got = exchange(send)
    terms, ends = edges(odd, first, second, count)
    ends = lax.ppermute(ends, "space", [(i, i ^ 1) for i in range(bands)])
    res, tan = stencil(first), stencil(second)
    table = basis(quad_nodes, degrees)
    scale = quad_weights * pressure_load * (STEEP * STEEP)
    table_w = (table.astype(F32) * scale[None, :]).astype(BF16)
    turn = one_hot(jnp.equal(*iotas((table.shape[0],) * 2))) * (-STEEP)
    table_t = lax.dot_general(table, turn.astype(BF16), (((0,), (0,)), ((), ())), preferred_element_type=F32).astype(BF16)
    shift = jnp.broadcast_to((STEEP * (gap_nominal - FLOOR))[:, None], (gap_nominal.shape[0], 128))
    terms, res, tan, table_t, table_w, shift = lax.optimization_barrier((terms, res, tan, table_t, table_w, shift))
    outer = lax.ppermute(terms, "space", [(i + a, i + b) for i in range(1, bands - 1, 2) for a, b in ((0, 1), (1, 0))])
    got, ends = lax.optimization_barrier((got, ends))
    force = quad_forces(got, table_t, table_w, shift)
    back = exchange(force)
    res, tan = add_outer(odd, outer, ends, res, tan, count)
    return tuple(merge(back, res, tan))


def solution(mesh):
    in_specs = (P("mode", "space", None), P("mode", "space", None), P(), P(), P(), P(), P())
    out_specs = (P("mode", "space", None), P("mode", "space", None))
    return jax.shard_map(shards, mesh=mesh, in_specs=in_specs, out_specs=out_specs, check_vma=False)
```
